256 devices in a mesh: view: 16 (over y, z_hi), seq: 16 (over z_lo, x, core).
Axes of the slice: x: 4, y: 4, z: 8 (z_hi: 4, z_lo: 2; z = z_hi * 2 + z_lo), core: 2. Of those that a mesh axis runs over, the one named last changes fastest.
Arguments:
- tokens: bfloat16 [32768, 2048], P(('view', 'seq')), may hold values from -6 to 6
- w_qkv: bfloat16 [2048, 6144], P(None, 'seq'), may hold values from -0.125 to 0.125
- w_out: bfloat16 [2048, 2048], P('seq'), may hold values from -0.125 to 0.125
- mod_shift: float32 [16, 2048], P('view'), may hold values from -3 to 3
- mod_scale: float32 [16, 2048], P('view'), may hold values from -1 to 11
- mod_gate: float32 [16, 2048], P('view'), may hold values from -4 to 4
- partners: int32 [16, 6], P('view'), may hold values from 0 to 15, as said below
- partner_count: int32 [16], P('view'), may hold values from 2 to 6
Outputs:
- result: bfloat16 [32768, 2048], P(('view', 'seq'))
The draws below stay inside these ranges and needn't reach their ends.
Inputs may be any that keep to these rules, and one draw needn't show every extreme that they name: partners[w, j] for j < partner_count[w] are distinct views other than w, each within 3 positions of w on the cyclic order of the 16 views; slots from partner_count[w] on hold w itself.
All inputs are finite; a program needn't handle non-finite values.
Results may differ from the reference program's by a relative error of at most 0.024.
The reference program's roundings to bfloat16 on the way (of `normed`, `joined` and `attended`) count: a program that leaves them out, or rounds other values in their place, can miss the bound.
Values may be sent and summed in bfloat16 or wider, within the bound.
A program may use at most 64 MiB of HBM per device.

```python
import jax
import jax.numpy as jnp
from jax import lax

D = 2048
HEADS = 16
HEAD_DIM = 128
FRAME_TOK = 256
MAXP = 6
VIEWS = 16
SEQ_LEN = 2048


def partner_table(key):
    key_count, key_order, key_pick = jax.random.split(key, 3)
    list_sizes = jax.random.randint(key_count, (VIEWS,), 2, MAXP + 1)
    chosen = jax.random.permutation(key_pick, VIEWS)
    list_sizes = list_sizes.at[chosen[0]].set(MAXP).at[chosen[1]].set(2)
    rank_keys = jax.random.randint(key_order, (VIEWS, 6), 0, 1 << 20) * 8 + jnp.arange(6, dtype=jnp.int32)[None, :]
    slot_order = jnp.argsort(rank_keys, axis=1)
    offset_table = jnp.array([1, -1, 2, -2, 3, -3], jnp.int32)
    own_view = jnp.arange(VIEWS, dtype=jnp.int32)[:, None]
    partner_ids = (own_view + offset_table[slot_order]) % VIEWS
    slot_ids = jnp.arange(MAXP, dtype=jnp.int32)[None, :]
    partner_ids = jnp.where(slot_ids < list_sizes[:, None], partner_ids, own_view)
    return (partner_ids.astype(jnp.int32), list_sizes.astype(jnp.int32))


def draw_partners(key, part):
    partner_ids, list_sizes = partner_table(key)
    return partner_ids


def draw_partner_count(key, part):
    partner_ids, list_sizes = partner_table(key)
    return list_sizes


def draw_mod_scale(key, part):
    key = jax.random.fold_in(key, 11)
    key_entry = jax.random.fold_in(key, 1)
    return jax.random.uniform(key_entry, (VIEWS, D), jnp.float32, -0.5, 0.5)


def shard_levels(own_key, shape, cuts, least, largest):
    factor_of, own = 1.0, jax.random.fold_in(own_key, 6)
    for axis_at, shards_of in cuts:
        steps = jnp.exp(jax.random.uniform(jax.random.fold_in(own, axis_at), (shards_of,), jnp.float32, least / len(cuts), largest / len(cuts)))
        factor_of = factor_of * jnp.repeat(steps, shape[axis_at] // shards_of).reshape([-1 if axis == axis_at else 1 for axis in range(len(shape))])
    return factor_of


def scatter_about(rng, dims, deviation, limit, cuts=(), held_as=jnp.bfloat16):
    values = jax.random.normal(rng, dims, jnp.float32) * deviation
    if len(cuts) > 0:
        values = shard_levels(rng, dims, cuts, -0.22, 0.18) * values
    return jnp.clip(values, min=-limit, max=limit).astype(held_as)


def setup_inputs(seed: int = 0) -> dict:
    key_list = jax.random.split(jax.random.key(seed), 9)
    tokens = scatter_about(key_list[0], (VIEWS * SEQ_LEN, D), 1.0, 6.0, ((0, 256),))
    w_qkv = scatter_about(key_list[1], (D, 3 * D), D ** -0.5, 0.125, ((1, 16),))
    w_out = scatter_about(key_list[2], (D, D), D ** -0.5, 0.125, ((0, 16),))
    mod_shift = scatter_about(key_list[3], (VIEWS, D), 0.5, 3.0, ((0, 16),), jnp.float32)
    mod_scale = draw_mod_scale(jax.random.fold_in(key_list[8], 71), 0)
    mod_gate = scatter_about(key_list[5], (VIEWS, D), 1.0, 4.0, ((0, 16),), jnp.float32)
    partners = draw_partners(jax.random.fold_in(key_list[8], 71), 0)
    partner_count = draw_partner_count(jax.random.fold_in(key_list[8], 71), 0)
    return dict(tokens=tokens, w_qkv=w_qkv, w_out=w_out, mod_shift=mod_shift, mod_scale=mod_scale, mod_gate=mod_gate, partners=partners, partner_count=partner_count)


EPS = 1e-06

def rounded(values):
    return lax.optimization_barrier(values.astype(jnp.bfloat16)).astype(jnp.float32)

def view_attention(queries, keyval, extra_kv, flags, frame_tok):
    seq_len, head_count, head_width = queries.shape
    frames = seq_len // frame_tok
    score_scale = head_width ** (-0.5)
    key_part = keyval[:, :, 0].astype(jnp.float32)
    val_part = keyval[:, :, 1].astype(jnp.float32)

    def one_frame(frame_index):
        first_row = frame_index * frame_tok
        frame_q = lax.dynamic_slice_in_dim(queries, first_row, frame_tok, 0).astype(jnp.float32)
        far_kv = lax.dynamic_slice_in_dim(extra_kv, first_row, frame_tok, 1).astype(jnp.float32)
        own_scores = jnp.einsum('qhe,khe->hqk', frame_q, key_part) * score_scale
        far_scores = jnp.einsum('qhe,pkhe->hqpk', frame_q, far_kv[:, :, :, 0]) * score_scale
        far_scores = jnp.where(flags[None, None, :, None], far_scores, -jnp.inf)
        row_max = jnp.maximum(own_scores.max(axis=-1), far_scores.max(axis=(-2, -1)))
        own_prob = jnp.exp(own_scores - row_max[..., None])
        far_prob = jnp.exp(far_scores - row_max[..., None, None])
        weight_sum = own_prob.sum(axis=-1) + far_prob.sum(axis=(-2, -1))
        weighted = jnp.einsum('hqk,khe->qhe', rounded(own_prob), val_part)
        weighted = weighted + jnp.einsum('hqpk,pkhe->qhe', rounded(far_prob), far_kv[:, :, :, 1])
        return (weighted / jnp.transpose(weight_sum)[:, :, None]).astype(jnp.bfloat16)
    framed = lax.map(one_frame, jnp.arange(frames))
    return framed.reshape(seq_len, head_count * head_width)

def reference(tokens, w_qkv, w_out, mod_shift, mod_scale, mod_gate, partners, partner_count):
    view_count = mod_shift.shape[0]
    seq_len = tokens.shape[0] // view_count
    tokens_f32 = tokens.astype(jnp.float32).reshape(view_count, seq_len, D)
    row_mean = lax.optimization_barrier(jnp.mean(tokens_f32, axis=2, keepdims=True))
    centred = tokens_f32 - row_mean
    row_var = lax.optimization_barrier(jnp.mean(centred * centred, axis=2, keepdims=True))
    normed = (centred * lax.rsqrt(row_var + EPS) * (1.0 + mod_scale[:, None, :]) + mod_shift[:, None, :]).astype(jnp.bfloat16)
    joined = jnp.dot(normed.reshape(view_count * seq_len, D), w_qkv, preferred_element_type=jnp.float32).astype(jnp.bfloat16)
    joined = joined.reshape(view_count, seq_len, HEADS, 3, HEAD_DIM)
    kv_all = joined[:, :, :, 1:]
    slot_ids = jnp.arange(MAXP)

    def one_view(view_id):
        extra_kv = kv_all[partners[view_id]]
        flags = slot_ids < partner_count[view_id]
        return view_attention(joined[view_id, :, :, 0], kv_all[view_id], extra_kv, flags, FRAME_TOK)
    attended = lax.map(one_view, jnp.arange(view_count))
    projected = jnp.dot(attended.reshape(view_count * seq_len, D), w_out, preferred_element_type=jnp.float32)
    projected = projected.reshape(view_count, seq_len, D)
    result = tokens_f32 + mod_gate[:, None, :] * projected
    return result.reshape(view_count * seq_len, D).astype(jnp.bfloat16)
```

```python
import functools

import jax
import jax.numpy as jnp
from jax import lax
from jax.experimental import pallas as pl
from jax.experimental.pallas import tpu as pltpu
from jax.sharding import PartitionSpec as P

HEAD_DIM = 128
FRAME_TOK = 256
D = 2048
EPS = 1e-06
NEG = -1e30
EXP_SCALE = HEAD_DIM ** (-0.5) * 1.4426950408889634
MESH = pl.DeviceIdType.MESH


def kernel(
    tok_ref,
    wq_ref,
    shift_ref,
    scale_ref,
    bias_ref,
    out_ref,
    normed,
    wbuf,
    biases,
    qbuf,
    kvw,
    kvx,
    abuf,
    attr,
    bias_s,
    bias_r,
    up_s,
    up_r,
    dn_s,
    dn_r,
    sib_s,
    sib_r,
    wx_s,
    wx_r,
    wy_s,
    wy_r,
    x_s,
    x_r,
    y_s,
    y_r,
    a_s,
    a_r,
    loc_s,
):
    w = lax.axis_index("view")
    s = lax.axis_index("seq")
    y, zh = w // 4, w % 4
    zl, x, c = s // 8, (s // 2) % 4, s % 2
    z = zh * 2 + zl

    def dev(x_, y_, z_, c_):
        return {"view": y_ * 4 + z_ // 2, "seq": (z_ % 2) * 8 + x_ * 2 + c_}

    def rcopy(src, dst, ss, rs, device):
        return pltpu.make_async_remote_copy(
            src_ref=src, dst_ref=dst, send_sem=ss, recv_sem=rs, device_id=device, device_id_type=MESH
        )

    def zdev(k, c_=None):
        return dev(x, y, (z + k) % 8, c if c_ is None else c_)

    def xdev(d):
        return dev((x + d) % 4, y, z, c)

    def ydev(d):
        return dev(x, (y + d) % 4, z, c)

    sib = dev(x, y, z, 1 - c)

    barrier = pltpu.get_barrier_semaphore()
    peers = [sib]
    for k in range(1, 8):
        peers += [zdev(k), zdev(k, 1 - c)]
    for d in range(1, 4):
        peers += [xdev(d), ydev(d)]
    for p in peers:
        pl.semaphore_signal(barrier, inc=1, device_id=p, device_id_type=MESH)

    t = tok_ref[...].astype(jnp.float32)
    t = t - jnp.mean(t, axis=1, keepdims=True)
    var = jnp.mean(t * t, axis=1, keepdims=True)
    normed[z, c] = (t * lax.rsqrt(var + EPS) * (1.0 + scale_ref[...]) + shift_ref[...]).astype(jnp.bfloat16)
    biases[zh] = bias_ref[...]

    pl.semaphore_wait(barrier, len(peers))

    quarter = wbuf.at[pl.ds(pl.multiple_of(y * 512, 512), 512)]
    my_quarter = wq_ref.at[pl.ds(pl.multiple_of(y * 512, 512), 512)]
    native = x == zh

    def wx_copy(d):
        return rcopy(my_quarter, quarter, wx_s.at[d - 1], wx_r, xdev(d))

    def wy_copy(d):
        return rcopy(quarter, quarter, wy_s.at[d - 1], wy_r.at[y], ydev(d))

    own_w = pltpu.make_async_copy(wq_ref, wbuf, loc_s)

    @pl.when(native)
    def _():
        for d in (1, 3, 2):
            wx_copy(d).start()
        own_w.start()

    def block(zz, cc, half):
        return normed.at[zz, cc, pl.ds(half * 64, 64)]

    def up_copy(k, half):
        b = block((z + 8 - k) % 8, c, half)
        return rcopy(b, b, up_s.at[k, half], up_r.at[k, half], zdev(1))

    def dn_copy(k, half):
        b = block((z + k) % 8, c, half)
        return rcopy(b, b, dn_s.at[k, half], dn_r.at[k, half], zdev(7))

    def sib_copy(k, half):
        b = block((z + k) % 8, c, half)
        return rcopy(b, b, sib_s.at[k, half], sib_r.at[k, half], sib)

    for half in (0, 1):
        up_copy(0, half).start()
        dn_copy(0, half).start()
    for half in (0, 1):
        sib_copy(0, half).start()

    def bias_copy(d):
        b = biases.at[zh]
        return rcopy(b, b, bias_s.at[d - 1], bias_r.at[d - 1], dev(x, y, (z + 2 * d) % 8, c))

    for d in range(1, 4):
        bias_copy(d).start()

    def event(k, half):
        if k < 4 or half == 0:
            up_copy(k - 1, half).wait_recv()
            if k < 3 or (k == 3 and half == 0):
                up_copy(k, half).start()
        if k < 4 or half == 1:
            dn_copy(k - 1, half).wait_recv()
            if k < 3 or (k == 3 and half == 1):
                dn_copy(k, half).start()
        if k < 4:
            sib_copy(8 - k, half).start()
            sib_copy(k, half).start()
        else:
            sib_copy(4, half).start()

    def x_copy(zz, d):
        v, fi = zz // 2, zz % 2
        return rcopy(kvw.at[fi, 3 + v], kvx.at[v, d - 1, fi], x_s.at[zz, d - 1], x_r.at[zz, d - 1], xdev(d))

    def yup_copy(zz):
        v, fi = zz // 2, zz % 2
        return rcopy(kvw.at[fi, 3 + v], kvw.at[fi, v - 1], y_s.at[zz, 0], y_r.at[fi, v - 1], ydev(1))

    def ydn_copy(zz):
        v, fi = zz // 2, zz % 2
        return rcopy(kvw.at[fi, 3 + v], kvw.at[fi, 7 + v], y_s.at[zz, 1], y_r.at[fi, 4 + v - 1], ydev(3))

    def unit(k):
        zz = (z + k) % 8
        for half in (0, 1):
            sib_copy(k, half).wait_recv()
        rows = normed[zz].reshape(256, D)
        joined = jnp.dot(rows, wbuf[...], preferred_element_type=jnp.float32).astype(jnp.bfloat16)
        qbuf[zz] = joined[:, :HEAD_DIM]
        kvw[zz % 2, 3 + zz // 2] = joined[:, HEAD_DIM:]
        for d in (1, 3, 2):
            x_copy(zz, d).start()

        @pl.when(zz >= 2)
        def _():
            yup_copy(zz).start()

        @pl.when(zz < 6)
        def _():
            ydn_copy(zz).start()

    event(1, 0)
    event(1, 1)

    @pl.when(jnp.logical_not(native))
    def _():
        wx_copy(1).wait_recv()
        for d in (1, 3, 2):
            wy_copy(d).start()

    event(2, 0)
    event(2, 1)

    @pl.when(native)
    def _():
        own_w.wait()

    @pl.when(jnp.logical_not(native))
    def _():
        for d in range(1, 4):
            q = (y + d) % 4
            rcopy(quarter, quarter, wy_s.at[0], wy_r.at[q], sib).wait_recv()

    unit(0)
    event(3, 0)
    unit(1)
    unit(7)
    event(3, 1)
    unit(2)
    unit(6)
    event(4, 0)
    event(4, 1)
    unit(3)
    unit(5)
    unit(4)

    def wait_unit(zz, carry):
        for d in range(1, 4):
            x_copy(zz, d).wait_recv()
        return carry

    lax.fori_loop(0, 8, wait_unit, 0)
    for fi in range(2):
        for slot in range(6):
            rcopy(kvw.at[fi, 0], kvw.at[fi, 0], y_s.at[0, 0], y_r.at[fi, slot], sib).wait_recv()
    for d in range(1, 4):
        bias_copy(d).wait_recv()

    head = zl * 8 + zh * 2 + c

    def a_copy(u, cc):
        return rcopy(
            abuf.at[u, pl.ds(cc * 128, 128)],
            attr.at[head],
            a_s.at[u, cc],
            a_r.at[head],
            dev(x, y, u, cc),
        )

    def attend(u, carry):
        v, fi = u // 2, u % 2
        q = qbuf[u]

        def score(kv):
            return lax.dot_general(
                q, kv[:, :HEAD_DIM], (((1,), (1,)), ((), ())), preferred_element_type=jnp.float32
            )

        kv_list = [kvw.at[1 - fi, 3 + v]]
        for d in range(3):
            for f in range(2):
                kv_list.append(kvx.at[v, d, f])
        for j in range(7):
            kv_list.append(kvw.at[fi, v + j])
        scores = []
        for i, kv in enumerate(kv_list):
            sc = score(kv)
            if i >= 7 and i != 10:
                row = biases[v, pl.ds(i - 7, 1), :]
                sc = sc + jnp.concatenate([row, row], axis=1)
            scores.append(sc)
        mx = functools.reduce(jnp.maximum, scores)
        mx = jnp.max(mx, axis=1, keepdims=True) * EXP_SCALE
        total = jnp.zeros((256, 256), jnp.float32)
        acc = jnp.zeros((256, HEAD_DIM), jnp.float32)
        for sc, kv in zip(scores, kv_list):
            p = jnp.exp2(sc * EXP_SCALE - mx)
            total = total + p
            acc = acc + jnp.dot(
                p.astype(jnp.bfloat16), kv[:, HEAD_DIM:], preferred_element_type=jnp.float32
            )
        den = jnp.sum(total, axis=1, keepdims=True)
        abuf[u] = (acc / den).astype(jnp.bfloat16)
        for cc in range(2):
            mine = jnp.logical_and(u == z, cc == c)

            @pl.when(mine)
            def _():
                attr[head] = abuf[u, pl.ds(cc * 128, 128)]

            @pl.when(jnp.logical_not(mine))
            def _():
                a_copy(u, cc).start()

        return carry

    lax.fori_loop(0, 8, attend, 0)

    for h in range(16):
        @pl.when(h != head)
        def _():
            rcopy(attr.at[h], attr.at[h], a_s.at[0, 0], a_r.at[h], sib).wait_recv()
        out_ref[:, h * 128 : (h + 1) * 128] = attr[h]

    for half in (0, 1):
        for k in range(3):
            up_copy(k, half).wait_send()
            dn_copy(k, half).wait_send()
        for k in range(8):
            if k != 4:
                sib_copy(k, half).wait_send()
    up_copy(3, 0).wait_send()
    dn_copy(3, 1).wait_send()
    for half in (0, 1):
        sib_copy(4, half).wait_send()
    for d in range(1, 4):
        bias_copy(d).wait_send()

    @pl.when(native)
    def _():
        for d in range(1, 4):
            wx_copy(d).wait_send()

    @pl.when(jnp.logical_not(native))
    def _():
        for d in range(1, 4):
            wy_copy(d).wait_send()

    def end_unit(zz, carry):
        for d in range(1, 4):
            x_copy(zz, d).wait_send()

        @pl.when(zz >= 2)
        def _():
            yup_copy(zz).wait_send()

        @pl.when(zz < 6)
        def _():
            ydn_copy(zz).wait_send()

        for cc in range(2):
            @pl.when(jnp.logical_not(jnp.logical_and(zz == z, cc == c)))
            def _():
                a_copy(zz, cc).wait_send()

        return carry

    lax.fori_loop(0, 8, end_unit, 0)


def per_device(tokens, w_qkv, w_out, mod_shift, mod_scale, mod_gate, partners, partner_count):
    me = lax.axis_index("view")
    views = lax.axis_size("view")
    w_full = lax.all_gather(w_out, "seq", axis=0, tiled=True)
    offset = jnp.arange(8) - 3
    target = (me + offset) % views
    used = jnp.arange(partners.shape[1])[None, :] < partner_count[0]
    flag = jnp.any((partners == target[:, None]) & used, axis=1)
    bias = jnp.broadcast_to(jnp.where(flag, 0.0, NEG)[:, None], (8, 128)).astype(jnp.float32)

    vmem = pl.BlockSpec(memory_space=pltpu.VMEM)
    bf16, f32 = jnp.bfloat16, jnp.float32
    dma = pltpu.SemaphoreType.DMA
    att = pl.pallas_call(
        kernel,
        out_shape=jax.ShapeDtypeStruct((128, D), bf16),
        in_specs=[vmem] * 5,
        out_specs=vmem,
        scratch_shapes=[
            pltpu.VMEM((8, 2, 128, D), bf16),
            pltpu.VMEM((D, 384), bf16),
            pltpu.VMEM((4, 8, 128), f32),
            pltpu.VMEM((8, 256, 128), bf16),
            pltpu.VMEM((2, 10, 256, 256), bf16),
            pltpu.VMEM((4, 3, 2, 256, 256), bf16),
            pltpu.VMEM((8, 256, 128), bf16),
            pltpu.VMEM((16, 128, 128), bf16),
            dma((3,)), dma((3,)),
            dma((4, 2)), dma((4, 2)),
            dma((4, 2)), dma((4, 2)),
            dma((8, 2)), dma((8, 2)),
            dma((3,)), dma,
            dma((3,)), dma((4,)),
            dma((8, 3)), dma((8, 3)),
            dma((8, 2)), dma((2, 6)),
            dma((8, 2)), dma((16,)),
            dma,
        ],
        compiler_params=pltpu.CompilerParams(
            collective_id=0, has_side_effects=True, vmem_limit_bytes=56 * 1024 * 1024
        ),
        cost_estimate=pl.CostEstimate(flops=8_000_000_000, bytes_accessed=30_000_000, transcendentals=7_000_000),
    )(tokens, w_qkv, mod_shift, mod_scale, bias)

    projected = jnp.dot(att, w_full, preferred_element_type=jnp.float32)
    return (tokens.astype(jnp.float32) + mod_gate * projected).astype(jnp.bfloat16)


def solution(mesh):
    in_specs = (
        P(("view", "seq"), None),
        P(None, "seq"),
        P("seq", None),
        P("view", None),
        P("view", None),
        P("view", None),
        P("view", None),
        P("view"),
    )
    out_specs = P(("view", "seq"), None)
    return jax.shard_map(
        per_device, mesh=mesh, in_specs=in_specs, out_specs=out_specs, check_vma=False
    )
```

```python
import functools

import jax
import jax.numpy as jnp
from jax import lax
from jax.experimental import pallas as pl
from jax.experimental.pallas import tpu as pltpu
from jax.sharding import PartitionSpec as P

HEAD_DIM = 128
FRAME_TOK = 256
D = 2048
EPS = 1e-06
NEG = -1e30
EXP_SCALE = HEAD_DIM ** (-0.5) * 1.4426950408889634
MESH = pl.DeviceIdType.MESH


def kernel(
    tok_ref,
    wq_ref,
    wo_ref,
    shift_ref,
    scale_ref,
    gate_ref,
    bias_ref,
    out_ref,
    normed,
    wbuf,
    biases,
    qbuf,
    kvw,
    kvx,
    abuf,
    attr,
    wout,
    bias_s,
    bias_r,
    up_s,
    up_r,
    dn_s,
    dn_r,
    sib_s,
    sib_r,
    wx_s,
    wx_r,
    wy_s,
    wy_r,
    x_s,
    x_r,
    f_s,
    f_r,
    y_s,
    y_r,
    a_s,
    a_r,
    ox_s,
    ox_r,
    oy_s,
    oy_r,
    oz_s,
    oz_r,
    os_s,
    os_r,
    loc_s,
):
    w = lax.axis_index("view")
    s = lax.axis_index("seq")
    y, zh = w // 4, w % 4
    zl, x, c = s // 8, (s // 2) % 4, s % 2
    z = zh * 2 + zl

    def dev(x_, y_, z_, c_):
        return {"view": y_ * 4 + z_ // 2, "seq": (z_ % 2) * 8 + x_ * 2 + c_}

    def rcopy(src, dst, ss, rs, device):
        return pltpu.make_async_remote_copy(
            src_ref=src, dst_ref=dst, send_sem=ss, recv_sem=rs, device_id=device, device_id_type=MESH
        )

    def zdev(k, c_=None):
        return dev(x, y, (z + k) % 8, c if c_ is None else c_)

    def xdev(d):
        return dev((x + d) % 4, y, z, c)

    def ydev(d):
        return dev(x, (y + d) % 4, z, c)

    sib = dev(x, y, z, 1 - c)

    barrier = pltpu.get_barrier_semaphore()
    peers = [sib]
    for k in range(1, 8):
        peers += [zdev(k), zdev(k, 1 - c)]
    for d in range(1, 4):
        peers += [xdev(d), ydev(d)]
    for p in peers:
        pl.semaphore_signal(barrier, inc=1, device_id=p, device_id_type=MESH)

    t = tok_ref[...].astype(jnp.float32)
    t = t - jnp.mean(t, axis=1, keepdims=True)
    var = jnp.mean(t * t, axis=1, keepdims=True)
    normed[z, c] = (t * lax.rsqrt(var + EPS) * (1.0 + scale_ref[...]) + shift_ref[...]).astype(jnp.bfloat16)
    biases[zh] = bias_ref[...]

    pl.semaphore_wait(barrier, len(peers))

    def piece(ref, p):
        return ref.at[pl.ds(pl.multiple_of(y * 512, 512), 512), pl.ds(p * 128, 128)]

    native = x == zh

    def wx_copy(p, d):
        return rcopy(piece(wq_ref, p), piece(wbuf, p), wx_s.at[p, d - 1], wx_r.at[p], xdev(d))

    def wy_copy(p, d):
        return rcopy(piece(wbuf, p), piece(wbuf, p), wy_s.at[p, d - 1], wy_r.at[p, y], ydev(d))

    def pass_weights(p):
        @pl.when(jnp.logical_not(native))
        def _():
            wx_copy(p, 1).wait_recv()
            for d in (1, 3, 2):
                wy_copy(p, d).start()

    def wait_weights(p):
        @pl.when(jnp.logical_not(native))
        def _():
            for d in range(1, 4):
                rcopy(piece(wbuf, p), piece(wbuf, p), wy_s.at[p, 0], wy_r.at[p, (y + d) % 4], sib).wait_recv()

    own_w = pltpu.make_async_copy(wq_ref, wbuf, loc_s.at[0])
    own_o = pltpu.make_async_copy(
        wo_ref, wout.at[c, zl, pl.ds(pl.multiple_of(x * 128, 128), 128)], loc_s.at[1]
    )
    own_o.start()

    @pl.when(native)
    def _():
        for p in (1, 2, 0):
            for d in (1, 3, 2):
                wx_copy(p, d).start()
        own_w.start()

    def block(zz, cc, half):
        return normed.at[zz, cc, pl.ds(half * 64, 64)]

    def up_copy(k, half):
        b = block((z + 8 - k) % 8, c, half)
        return rcopy(b, b, up_s.at[k, half], up_r.at[k, half], zdev(1))

    def dn_copy(k, half):
        b = block((z + k) % 8, c, half)
        return rcopy(b, b, dn_s.at[k, half], dn_r.at[k, half], zdev(7))

    def sib_copy(k, half):
        b = block((z + k) % 8, c, half)
        return rcopy(b, b, sib_s.at[k, half], sib_r.at[k, half], sib)

    for half in (0, 1):
        up_copy(0, half).start()
        dn_copy(0, half).start()
    for half in (0, 1):
        sib_copy(0, half).start()

    def bias_copy(d):
        b = biases.at[zh]
        return rcopy(b, b, bias_s.at[d - 1], bias_r.at[d - 1], dev(x, y, (z + 2 * d) % 8, c))

    for d in range(1, 4):
        bias_copy(d).start()

    def event(k, half):
        if k < 4 or half == 0:
            up_copy(k - 1, half).wait_recv()
            if k < 3 or (k == 3 and half == 0):
                up_copy(k, half).start()
        if k < 4 or half == 1:
            dn_copy(k - 1, half).wait_recv()
            if k < 3 or (k == 3 and half == 1):
                dn_copy(k, half).start()
        if k < 4:
            sib_copy(8 - k, half).start()
            sib_copy(k, half).start()
        else:
            sib_copy(4, half).start()

    def x_copy(zz, d):
        v, fi = zz // 2, zz % 2
        return rcopy(kvw.at[fi, 3 + v], kvx.at[v, d - 1, fi], x_s.at[zz, d - 1], x_r.at[zz, d - 1], xdev(d))

    def f_copy(zz, half, direct):
        v, fi = zz // 2, zz % 2
        rows = pl.ds(half * 128, 128)
        src = kvw.at[fi, 3 + v, rows] if direct else kvx.at[v, 2 * half, fi, rows]
        to = xdev(2) if direct else xdev(1 + 2 * half)
        return rcopy(src, kvx.at[v, 1, fi, rows], f_s.at[zz, half], f_r.at[zz, half], to)

    def forward(k):
        zz = (z + k) % 8
        for half in (0, 1):
            x_copy(zz, 1 + 2 * half).wait_recv()
            f_copy(zz, half, False).start()

    def yup_copy(zz):
        v, fi = zz // 2, zz % 2
        return rcopy(kvw.at[fi, 3 + v], kvw.at[fi, v - 1], y_s.at[zz, 0], y_r.at[fi, v - 1], ydev(1))

    def ydn_copy(zz):
        v, fi = zz // 2, zz % 2
        return rcopy(kvw.at[fi, 3 + v], kvw.at[fi, 7 + v], y_s.at[zz, 1], y_r.at[fi, 4 + v - 1], ydev(3))

    def rows_of(k):
        return normed[(z + k) % 8].reshape(256, D)

    def kv_unit(k):
        zz = (z + k) % 8
        for half in (0, 1):
            sib_copy(k, half).wait_recv()
        kv = jnp.dot(rows_of(k), wbuf[:, HEAD_DIM:], preferred_element_type=jnp.float32)
        kvw[zz % 2, 3 + zz // 2] = kv.astype(jnp.bfloat16)
        for d in (1, 3):
            x_copy(zz, d).start()
        if k == 4:
            for half in (0, 1):
                f_copy(zz, half, True).start()

        @pl.when(zz >= 2)
        def _():
            yup_copy(zz).start()

        @pl.when(zz < 6)
        def _():
            ydn_copy(zz).start()

    def q_unit(k):
        q = jnp.dot(rows_of(k), wbuf[:, :HEAD_DIM], preferred_element_type=jnp.float32)
        qbuf[(z + k) % 8] = q.astype(jnp.bfloat16)

    par = y % 2

    def wrows(xx, first, count):
        return pl.ds(pl.multiple_of(xx * 128 + first, count), count)

    def ox_copy(d):
        return rcopy(
            wo_ref.at[pl.ds(pl.multiple_of(par * 64, 64), 64)],
            wout.at[c, zl, wrows(x, par * 64, 64)],
            ox_s.at[d - 1],
            ox_r.at[d - 1],
            xdev(d),
        )

    def oy_copy(d, up):
        b = wout.at[c, zl, wrows((x + d) % 4, par * 64 + (1 - up) * 32, 32)]
        return rcopy(b, b, oy_s.at[d - 1, up], oy_r.at[d - 1, up], ydev(1 if up else 3))

    def oz_copy(up):
        b = wout.at[c, zl, pl.ds((1 - up) * 256, 256)]
        return rcopy(b, b, oz_s.at[up], oz_r.at[up], zdev(1 if up else 7))

    def os_copy(i):
        b = wout.at[c, zl] if i == 2 else wout.at[c, 1 - zl, pl.ds((1 - i) * 256, 256)]
        return rcopy(b, b, os_s.at[i], os_r.at[i], sib)

    pass_weights(1)
    event(1, 0)
    pass_weights(2)
    event(1, 1)
    pass_weights(0)
    for d in (1, 3, 2):
        ox_copy(d).start()
    event(2, 0)

    @pl.when(native)
    def _():
        own_w.wait()

    wait_weights(1)
    wait_weights(2)
    kv_unit(0)
    kv_unit(1)
    kv_unit(7)
    event(2, 1)
    kv_unit(2)
    kv_unit(6)
    wait_weights(0)
    q_unit(0)
    q_unit(1)
    q_unit(7)
    event(3, 0)
    forward(0)
    for d in range(1, 4):
        ox_copy(d).wait_recv()
    for d in range(1, 4):
        for up in (1, 0):
            oy_copy(d, up).start()
    q_unit(2)
    q_unit(6)
    event(3, 1)
    kv_unit(3)
    kv_unit(5)
    forward(1)
    forward(7)
    event(4, 0)
    event(4, 1)
    kv_unit(4)
    own_o.wait()
    for d in range(1, 4):
        for up in (1, 0):
            oy_copy(d, up).wait_recv()
    for up in (1, 0):
        oz_copy(up).start()
    os_copy(2).start()
    forward(2)
    forward(6)
    q_unit(3)
    q_unit(5)
    q_unit(4)
    forward(3)
    forward(5)

    for half in (0, 1):
        x_copy((z + 4) % 8, 1 + 2 * half).wait_recv()

    def wait_unit(zz, carry):
        for half in (0, 1):
            f_copy(zz, half, False).wait_recv()
        return carry

    lax.fori_loop(0, 8, wait_unit, 0)
    for fi in range(2):
        for slot in range(6):
            rcopy(kvw.at[fi, 0], kvw.at[fi, 0], y_s.at[0, 0], y_r.at[fi, slot], sib).wait_recv()
    for d in range(1, 4):
        bias_copy(d).wait_recv()

    head = zl * 8 + zh * 2 + c

    def acols(h):
        return attr.at[(h % 2) * 2 + h // 8, :, pl.ds(pl.multiple_of((h // 2) % 4 * 128, 128), 128)]

    def a_copy(u, cc):
        return rcopy(
            abuf.at[u, pl.ds(cc * 128, 128)],
            acols(head),
            a_s.at[u, cc],
            a_r.at[head],
            dev(x, y, u, cc),
        )

    def attend(u, carry):
        v, fi = u // 2, u % 2
        q = qbuf[u]

        def score(kv):
            return lax.dot_general(
                q, kv[:, :HEAD_DIM], (((1,), (1,)), ((), ())), preferred_element_type=jnp.float32
            )

        kv_list = [kvw.at[1 - fi, 3 + v]]
        for d in range(3):
            for f in range(2):
                kv_list.append(kvx.at[v, d, f])
        for j in range(7):
            kv_list.append(kvw.at[fi, v + j])
        scores = []
        for i, kv in enumerate(kv_list):
            sc = score(kv)
            if i >= 7 and i != 10:
                row = biases[v, pl.ds(i - 7, 1), :]
                sc = sc + jnp.concatenate([row, row], axis=1)
            scores.append(sc)
        mx = functools.reduce(jnp.maximum, scores)
        mx = jnp.max(mx, axis=1, keepdims=True) * EXP_SCALE
        total = jnp.zeros((256, 256), jnp.float32)
        acc = jnp.zeros((256, HEAD_DIM), jnp.float32)
        for sc, kv in zip(scores, kv_list):
            p = jnp.exp2(sc * EXP_SCALE - mx)
            total = total + p
            acc = acc + jnp.dot(
                p.astype(jnp.bfloat16), kv[:, HEAD_DIM:], preferred_element_type=jnp.float32
            )
        den = jnp.sum(total, axis=1, keepdims=True)
        abuf[u] = (acc / den).astype(jnp.bfloat16)
        for cc in range(2):
            mine = jnp.logical_and(u == z, cc == c)

            @pl.when(mine)
            def _():
                acols(head)[...] = abuf[u, pl.ds(cc * 128, 128)]

            @pl.when(jnp.logical_not(mine))
            def _():
                a_copy(u, cc).start()

        return carry

    lax.fori_loop(0, 8, attend, 0)

    for up in (1, 0):
        oz_copy(up).wait_recv()
        os_copy(up).start()
    for i in range(3):
        os_copy(i).wait_recv()
    for h in range(16):
        @pl.when(h != head)
        def _():
            rcopy(acols(h), acols(h), a_s.at[0, 0], a_r.at[h], sib).wait_recv()

    def project(j, carry):
        cols = pl.ds(pl.multiple_of(j * 256, 256), 256)
        acc = jnp.zeros((128, 256), jnp.float32)
        for cc in range(2):
            for ll in range(2):
                acc = acc + jnp.dot(
                    attr[cc * 2 + ll], wout[cc, ll, :, cols], preferred_element_type=jnp.float32
                )
        out_ref[:, cols] = (
            tok_ref[:, cols].astype(jnp.float32) + gate_ref[:, cols] * acc
        ).astype(jnp.bfloat16)
        return carry

    lax.fori_loop(0, 8, project, 0)

    for half in (0, 1):
        for k in range(3):
            up_copy(k, half).wait_send()
            dn_copy(k, half).wait_send()
        for k in range(8):
            if k != 4:
                sib_copy(k, half).wait_send()
    up_copy(3, 0).wait_send()
    dn_copy(3, 1).wait_send()
    for half in (0, 1):
        sib_copy(4, half).wait_send()
    for d in range(1, 4):
        bias_copy(d).wait_send()
        ox_copy(d).wait_send()
        for up in (1, 0):
            oy_copy(d, up).wait_send()
    for up in (1, 0):
        oz_copy(up).wait_send()
    for i in range(3):
        os_copy(i).wait_send()

    @pl.when(native)
    def _():
        for p in range(3):
            for d in range(1, 4):
                wx_copy(p, d).wait_send()

    @pl.when(jnp.logical_not(native))
    def _():
        for p in range(3):
            for d in range(1, 4):
                wy_copy(p, d).wait_send()

    def end_unit(zz, carry):
        for half in (0, 1):
            x_copy(zz, 1 + 2 * half).wait_send()
            f_copy(zz, half, False).wait_send()

        @pl.when(zz >= 2)
        def _():
            yup_copy(zz).wait_send()

        @pl.when(zz < 6)
        def _():
            ydn_copy(zz).wait_send()

        for cc in range(2):
            @pl.when(jnp.logical_not(jnp.logical_and(zz == z, cc == c)))
            def _():
                a_copy(zz, cc).wait_send()

        return carry

    lax.fori_loop(0, 8, end_unit, 0)


def per_device(tokens, w_qkv, w_out, mod_shift, mod_scale, mod_gate, partners, partner_count):
    me = lax.axis_index("view")
    views = lax.axis_size("view")
    offset = jnp.arange(8) - 3
    target = (me + offset) % views
    used = jnp.arange(partners.shape[1])[None, :] < partner_count[0]
    flag = jnp.any((partners == target[:, None]) & used, axis=1)
    bias = jnp.broadcast_to(jnp.where(flag, 0.0, NEG)[:, None], (8, 128)).astype(jnp.float32)

    vmem = pl.BlockSpec(memory_space=pltpu.VMEM)
    bf16, f32 = jnp.bfloat16, jnp.float32
    dma = pltpu.SemaphoreType.DMA
    return pl.pallas_call(
        kernel,
        out_shape=jax.ShapeDtypeStruct((128, D), bf16),
        in_specs=[vmem] * 7,
        out_specs=vmem,
        scratch_shapes=[
            pltpu.VMEM((8, 2, 128, D), bf16),
            pltpu.VMEM((D, 384), bf16),
            pltpu.VMEM((4, 8, 128), f32),
            pltpu.VMEM((8, 256, 128), bf16),
            pltpu.VMEM((2, 10, 256, 256), bf16),
            pltpu.VMEM((4, 3, 2, 256, 256), bf16),
            pltpu.VMEM((8, 256, 128), bf16),
            pltpu.VMEM((4, 128, 512), bf16),
            pltpu.VMEM((2, 2, 512, D), bf16),
            dma((3,)), dma((3,)),
            dma((4, 2)), dma((4, 2)),
            dma((4, 2)), dma((4, 2)),
            dma((8, 2)), dma((8, 2)),
            dma((3, 3)), dma((3,)),
            dma((3, 3)), dma((3, 4)),
            dma((8, 3)), dma((8, 3)),
            dma((8, 2)), dma((8, 2)),
            dma((8, 2)), dma((2, 6)),
            dma((8, 2)), dma((16,)),
            dma((3,)), dma((3,)),
            dma((3, 2)), dma((3, 2)),
            dma((2,)), dma((2,)),
            dma((3,)), dma((3,)),
            dma((2,)),
        ],
        compiler_params=pltpu.CompilerParams(
            collective_id=0, has_side_effects=True, vmem_limit_bytes=56 * 1024 * 1024
        ),
        cost_estimate=pl.CostEstimate(flops=8_000_000_000, bytes_accessed=30_000_000, transcendentals=7_000_000),
    )(tokens, w_qkv, w_out, mod_shift, mod_scale, mod_gate, bias)


def solution(mesh):
    in_specs = (
        P(("view", "seq"), None),
        P(None, "seq"),
        P("seq", None),
        P("view", None),
        P("view", None),
        P("view", None),
        P("view", None),
        P("view"),
    )
    out_specs = P(("view", "seq"), None)
    return jax.shard_map(
        per_device, mesh=mesh, in_specs=in_specs, out_specs=out_specs, check_vma=False
    )
```

```python
import functools

import jax
import jax.numpy as jnp
from jax import lax
from jax.experimental import pallas as pl
from jax.experimental.pallas import tpu as pltpu
from jax.sharding import PartitionSpec as P

HEAD_DIM = 128
FRAME_TOK = 256
D = 2048
EPS = 1e-06
NEG = -1e30
EXP_SCALE = HEAD_DIM ** (-0.5) * 1.4426950408889634
MESH = pl.DeviceIdType.MESH


def kernel(
    tok_ref,
    wq_ref,
    wo_ref,
    shift_ref,
    scale_ref,
    gate_ref,
    partners_ref,
    count_ref,
    out_ref,
    normed,
    wbuf,
    biases,
    qbuf,
    kvw,
    kvx,
    abuf,
    attr,
    wout,
    m_st,
    l_st,
    acc_st,
    bias_s,
    bias_r,
    up_s,
    up_r,
    dn_s,
    dn_r,
    sib_s,
    sib_r,
    wx_s,
    wx_r,
    wy_s,
    wy_r,
    x_s,
    x_r,
    f_s,
    f_r,
    y_s,
    y_r,
    a_s,
    a_r,
    ox_s,
    ox_r,
    oy_s,
    oy_r,
    oz_s,
    oz_r,
    ow_s,
    ow_r,
    os_s,
    os_r,
    loc_s,
):
    w = lax.axis_index("view")
    s = lax.axis_index("seq")
    y, zh = lax.div(w, 4), lax.rem(w, 4)
    zl, x, c = lax.div(s, 8), lax.rem(lax.div(s, 2), 4), lax.rem(s, 2)
    z = zh * 2 + zl
    unit_z = [lax.rem(z + k, 8) for k in range(8)]
    unit_v = [lax.div(u, 2) for u in unit_z]
    unit_f = [lax.rem(u, 2) for u in unit_z]
    next_x = [lax.rem(x + d, 4) for d in range(4)]
    next_y = [lax.rem(y + d, 4) for d in range(4)]
    z_dev = [
        [{"view": y * 4 + v, "seq": f * 8 + x * 2 + cc} for cc in (c, 1 - c)]
        for v, f in zip(unit_v, unit_f)
    ]
    x_dev = [{"view": w, "seq": zl * 8 + xx * 2 + c} for xx in next_x]
    y_dev = [{"view": yy * 4 + zh, "seq": s} for yy in next_y]
    sib = z_dev[0][1]

    def rcopy(src, dst, ss, rs, device):
        return pltpu.make_async_remote_copy(
            src_ref=src, dst_ref=dst, send_sem=ss, recv_sem=rs, device_id=device, device_id_type=MESH
        )

    barrier = pltpu.get_barrier_semaphore()
    peers = [sib] + [p for k in range(1, 8) for p in z_dev[k]] + x_dev[1:] + y_dev[1:]
    for p in peers:
        pl.semaphore_signal(barrier, inc=1, device_id=p, device_id_type=MESH)

    t = tok_ref[...].astype(jnp.float32)
    t = t - jnp.mean(t, axis=1, keepdims=True)
    var = jnp.mean(t * t, axis=1, keepdims=True)
    normed[z, c] = (t * lax.rsqrt(var + EPS) * (1.0 + scale_ref[...]) + shift_ref[...]).astype(jnp.bfloat16)

    pl.semaphore_wait(barrier, len(peers))

    def block(zz, cc, half):
        return normed.at[zz, cc, pl.ds(half * 64, 64)]

    def up_copy(k, half):
        b = block(unit_z[(8 - k) % 8], c, half)
        return rcopy(b, b, up_s.at[k, half], up_r.at[k, half], z_dev[1][0])

    def dn_copy(k, half):
        b = block(unit_z[k], c, half)
        return rcopy(b, b, dn_s.at[k, half], dn_r.at[k, half], z_dev[7][0])

    def sib_copy(k, half):
        b = block(unit_z[k], c, half)
        return rcopy(b, b, sib_s.at[k, half], sib_r.at[k, half], sib)

    for half in (0, 1):
        up_copy(0, half).start()
        dn_copy(0, half).start()
    for half in (0, 1):
        sib_copy(0, half).start()

    def piece(ref, p):
        return ref.at[pl.ds(pl.multiple_of(y * 512, 512), 512), pl.ds(p * 128, 128)]

    native = x == zh

    def wx_copy(p, d):
        return rcopy(piece(wq_ref, p), piece(wbuf, p), wx_s.at[p, d - 1], wx_r.at[p], x_dev[d])

    def wy_copy(p, d):
        return rcopy(piece(wbuf, p), piece(wbuf, p), wy_s.at[p, d - 1], wy_r.at[p, y], y_dev[d])

    def pass_weights(p):
        @pl.when(jnp.logical_not(native))
        def _():
            wx_copy(p, 1).wait_recv()
            for d in (1, 3, 2):
                wy_copy(p, d).start()

    def wait_weights(p):
        @pl.when(jnp.logical_not(native))
        def _():
            for d in range(1, 4):
                rcopy(piece(wbuf, p), piece(wbuf, p), wy_s.at[p, 0], wy_r.at[p, next_y[d]], sib).wait_recv()

    own_w = pltpu.make_async_copy(wq_ref, wbuf, loc_s.at[0])
    own_o = pltpu.make_async_copy(wo_ref, wout.at[c, zl, x], loc_s.at[1])
    own_o.start()

    @pl.when(native)
    def _():
        for p in (1, 2, 0):
            for d in (1, 3, 2):
                wx_copy(p, d).start()
        own_w.start()

    for j in range(7):
        if j != 3:
            target = lax.rem(w + j + 13, 16)
            hits = 0.0
            for slot in range(6):
                hit = jnp.logical_and(partners_ref[0, slot] == target, count_ref[0] > slot)
                hits = hits + jnp.where(hit, 1.0, 0.0)
            biases[zh, j : j + 1, :] = jnp.full((1, 128), jnp.where(hits > 0.0, 0.0, NEG), jnp.float32)
    m_st[...] = jnp.full(m_st.shape, NEG, jnp.float32)
    l_st[...] = jnp.zeros(l_st.shape, jnp.float32)
    acc_st[...] = jnp.zeros(acc_st.shape, jnp.float32)

    def bias_copy(d):
        b = biases.at[zh]
        return rcopy(b, b, bias_s.at[d - 1], bias_r.at[d - 1], z_dev[2 * d][0])

    for d in range(1, 4):
        bias_copy(d).start()

    def event(k, half):
        if k < 4 or half == 0:
            up_copy(k - 1, half).wait_recv()
            if k < 3 or (k == 3 and half == 0):
                up_copy(k, half).start()
        if k < 4 or half == 1:
            dn_copy(k - 1, half).wait_recv()
            if k < 3 or (k == 3 and half == 1):
                dn_copy(k, half).start()
        if k < 4:
            sib_copy(8 - k, half).start()
            sib_copy(k, half).start()
        else:
            sib_copy(4, half).start()

    def x_copy(k, d):
        zz, v, fi = unit_z[k], unit_v[k], unit_f[k]
        return rcopy(kvw.at[fi, 3 + v], kvx.at[v, d - 1, fi], x_s.at[zz, d - 1], x_r.at[zz, d - 1], x_dev[d])

    def f_copy(k, half):
        zz, v, fi = unit_z[k], unit_v[k], unit_f[k]
        rows = pl.ds(half * 128, 128)
        src = kvw.at[fi, 3 + v, rows] if k == 4 else kvx.at[v, 2 * half, fi, rows]
        to = x_dev[2] if k == 4 else x_dev[1 + 2 * half]
        return rcopy(src, kvx.at[v, 1, fi, rows], f_s.at[zz, half], f_r.at[zz, half], to)

    def forward(k):
        for half in (0, 1):
            x_copy(k, 1 + 2 * half).wait_recv()
            f_copy(k, half).start()

    def yup_copy(k):
        zz, v, fi = unit_z[k], unit_v[k], unit_f[k]
        return rcopy(kvw.at[fi, 3 + v], kvw.at[fi, v - 1], y_s.at[zz, 0], y_r.at[fi, v - 1], y_dev[1])

    def ydn_copy(k):
        zz, v, fi = unit_z[k], unit_v[k], unit_f[k]
        return rcopy(kvw.at[fi, 3 + v], kvw.at[fi, 7 + v], y_s.at[zz, 1], y_r.at[fi, 3 + v], y_dev[3])

    def y_both(k, act):
        @pl.when(unit_z[k] >= 2)
        def _():
            act(yup_copy(k))

        @pl.when(unit_z[k] < 6)
        def _():
            act(ydn_copy(k))

    def kv_unit(k):
        for half in (0, 1):
            sib_copy(k, half).wait_recv()
        rows = normed[unit_z[k]].reshape(256, D)
        kv = jnp.dot(rows, wbuf[:, HEAD_DIM:], preferred_element_type=jnp.float32)
        kvw[unit_f[k], 3 + unit_v[k]] = kv.astype(jnp.bfloat16)
        for d in (1, 3):
            x_copy(k, d).start()
        if k == 4:
            for half in (0, 1):
                f_copy(k, half).start()
        y_both(k, lambda copy: copy.start())

    def q_unit(k):
        rows = normed[unit_z[k]].reshape(256, D)
        q = jnp.dot(rows, wbuf[:, :HEAD_DIM], preferred_element_type=jnp.float32)
        qbuf[unit_z[k]] = q.astype(jnp.bfloat16)

    par = lax.rem(y, 2)
    half_rows = pl.ds(pl.multiple_of(par * 64, 64), 64)

    def quarter_rows(up):
        return pl.ds(pl.multiple_of(par * 64 + (1 - up) * 32, 32), 32)

    def ox_copy(d):
        return rcopy(
            wo_ref.at[half_rows], wout.at[c, zl, x, half_rows], ox_s.at[d - 1], ox_r.at[d - 1], x_dev[d]
        )

    def oy_copy(d, up):
        b = wout.at[c, zl, next_x[d], quarter_rows(up)]
        return rcopy(b, b, oy_s.at[d - 1, up], oy_r.at[d - 1, up], y_dev[1 if up else 3])

    def drain_w_out():
        for d in range(1, 4):
            ox_copy(d).wait_send()
            for up in (1, 0):
                oy_copy(d, up).wait_send()

    def oz_copy(up):
        b = wout.at[c, zl, pl.ds((1 - up) * 2, 2), half_rows]
        return rcopy(b, b, oz_s.at[up], oz_r.at[up], z_dev[1 if up else 7][0])

    def ow_copy(pair, up):
        b = wout.at[c, 1 - zl, pl.ds(pair * 2, 2), quarter_rows(up)]
        return rcopy(b, b, ow_s.at[pair, up], ow_r.at[pair, up], y_dev[1 if up else 3])

    def os_copy(i):
        b = wout.at[c, zl] if i == 2 else wout.at[c, 1 - zl, pl.ds(i * 2, 2)]
        return rcopy(b, b, os_s.at[i], os_r.at[i], sib)

    @pl.when(jnp.logical_not(native))
    def _():
        for d in (1, 3, 2):
            ox_copy(d).start()

    pass_weights(1)
    event(1, 0)
    pass_weights(2)
    event(1, 1)
    pass_weights(0)

    @pl.when(native)
    def _():
        for p in range(3):
            for d in range(1, 4):
                wx_copy(p, d).wait_send()
        for d in (1, 3, 2):
            ox_copy(d).start()
        own_w.wait()

    def acols(cc, ll, xx):
        return attr.at[cc * 2 + ll, :, pl.ds(pl.multiple_of(xx * 128, 128), 128)]

    def a_copy(k, other):
        cc = 1 - c if other else c
        return rcopy(
            abuf.at[unit_z[k], pl.ds(pl.multiple_of(cc * 128, 128), 128)],
            acols(c, zl, zh),
            a_s.at[k, other],
            a_r.at[k, other],
            z_dev[k][other],
        )

    def a_wait(k, other):
        src = acols(1 - c if other else c, unit_f[(8 - k) % 8], unit_v[(8 - k) % 8])
        return rcopy(src, src, a_s.at[k, other], a_r.at[k, other], sib)

    def finish(ks):
        for k in ks:
            u = unit_z[k]
            den = jnp.sum(l_st[u], axis=1, keepdims=True)
            abuf[u] = (acc_st[u] / den).astype(jnp.bfloat16)
        for k in ks:
            if k == 0:
                acols(c, zl, zh)[...] = abuf[z, pl.ds(pl.multiple_of(c * 128, 128), 128)]
            else:
                a_copy(k, 0).start()
            a_copy(k, 1).start()

    def groups(parts):
        first = []
        for u, blocks in parts:
            q = qbuf[u]
            scores = []
            for kv, row in blocks:
                sc = lax.dot_general(
                    q, kv[:, :HEAD_DIM], (((1,), (1,)), ((), ())), preferred_element_type=jnp.float32
                )
                if row is not None:
                    b = biases[lax.div(u, 2), pl.ds(row, 1), :]
                    sc = sc + jnp.concatenate([b, b], axis=1)
                scores.append(sc)
            mx = functools.reduce(jnp.maximum, scores)
            mx = jnp.max(mx, axis=1, keepdims=True) * EXP_SCALE
            m_old = m_st[u]
            m_new = jnp.maximum(m_old, mx)
            first.append((scores, m_new, jnp.exp2(m_old - m_new)))
        second = []
        for (u, blocks), (scores, m_new, alpha) in zip(parts, first):
            m_two = jnp.concatenate([m_new, m_new], axis=1)
            total = jnp.zeros((256, 256), jnp.float32)
            acc = jnp.zeros((256, HEAD_DIM), jnp.float32)
            for sc, (kv, row) in zip(scores, blocks):
                p = jnp.exp2(sc * EXP_SCALE - m_two)
                total = total + p
                acc = acc + jnp.dot(
                    p.astype(jnp.bfloat16), kv[:, HEAD_DIM:], preferred_element_type=jnp.float32
                )
            second.append((total, acc))
        for (u, blocks), (scores, m_new, alpha), (total, acc) in zip(parts, first, second):
            m_st[u] = m_new
            l_st[u] = l_st[u] * alpha + total[:, :128] + total[:, 128:]
            acc_st[u] = acc_st[u] * alpha + acc

    def own_view(v):
        parts = []
        for fi in range(2):
            blocks = [(kvw.at[fi, 3 + v], None), (kvw.at[1 - fi, 3 + v], None)]
            blocks += [(kvx.at[v, d, f], None) for d in range(3) for f in range(2)]
            parts.append((2 * v + fi, blocks))
        groups(parts)

    def window(v, fi, deltas):
        blocks = [(kvw.at[fi, v + o], o) for delta in deltas for o in (delta - 1, delta + 3)]
        return 2 * v + fi, blocks

    def wait_x(k):
        for half in (0, 1):
            f_copy(k, half).wait_recv()
        if k == 4:
            for half in (0, 1):
                x_copy(k, 1 + 2 * half).wait_recv()

    def wait_y(k):
        y_both(k, lambda copy: copy.wait_recv())

    sign = 1 - 2 * zl
    view_b, view_c, view_d = lax.rem(zh + 4 - sign, 4), lax.rem(zh + 4 + sign, 4), unit_v[4]
    views = [unit_v[6], zh, unit_v[2]]
    gaps = [3, 2, 1]

    wait_weights(1)
    wait_weights(2)
    kv_unit(0)
    event(2, 0)
    kv_unit(1)
    kv_unit(7)
    wait_weights(0)
    event(2, 1)
    kv_unit(2)
    kv_unit(6)
    for k in (0, 1, 7):
        q_unit(k)
    forward(0)
    event(3, 0)
    for d in range(1, 4):
        ox_copy(d).wait_recv()
    for d in range(1, 4):
        for up in (1, 0):
            oy_copy(d, up).start()
    q_unit(2)
    q_unit(6)
    forward(1)
    forward(7)
    for half in (0, 1):
        for k in range(2):
            up_copy(k, half).wait_send()
            dn_copy(k, half).wait_send()
        for k in (0, 1, 7):
            sib_copy(k, half).wait_send()
    for d in range(1, 4):
        bias_copy(d).wait_send()
        bias_copy(d).wait_recv()

    @pl.when(jnp.logical_not(native))
    def _():
        for p in range(3):
            for d in range(1, 4):
                wy_copy(p, d).wait_send()

    event(3, 1)
    kv_unit(3)
    kv_unit(5)
    q_unit(3)
    q_unit(5)
    forward(2)
    forward(6)
    for d in range(1, 4):
        for up in (1, 0):
            oy_copy(d, up).wait_recv()
    own_o.wait()
    for up in (1, 0):
        oz_copy(up).start()
    for k in (0, 1, 7):
        wait_x(k)
    own_view(zh)
    for k in (0, 1, 7):
        for half in (0, 1):
            x_copy(k, 1 + 2 * half).wait_send()
            f_copy(k, half).wait_send()
        y_both(k, lambda copy: copy.wait_send())
    event(4, 0)
    event(4, 1)
    kv_unit(4)
    forward(3)
    forward(5)
    q_unit(4)
    os_copy(2).start()
    wait_x(2)
    wait_x(6)
    own_view(view_b)
    for k in (1, 7, 3, 5):
        wait_y(k)
    groups([window(unit_v[k], 1 - zl, (1, 2, 3)) for k in (1, 3, 5, 7)])
    finish((1, 7))
    for k in (0, 2, 6):
        wait_y(k)
    groups([window(v, zl, [e for e in (1, 2, 3) if e != g]) for v, g in zip(views, gaps)])
    for pair in (0, 1):
        oz_copy(1 - pair).wait_recv()
        for up in (1, 0):
            ow_copy(pair, up).start()
    wait_y(4)
    groups(
        [window(v, zl, (g,)) for v, g in zip(views, gaps)] + [window(view_d, zl, (1, 2, 3))]
    )
    wait_x(3)
    wait_x(5)
    own_view(view_c)
    finish((0, 2, 6))

    @pl.when(zl == 0)
    def _():
        finish((3,))

    @pl.when(zl == 1)
    def _():
        finish((5,))

    wait_x(4)
    own_view(view_d)

    @pl.when(zl == 0)
    def _():
        finish((5,))

    @pl.when(zl == 1)
    def _():
        finish((3,))

    finish((4,))

    for half in (0, 1):
        up_copy(2, half).wait_send()
        dn_copy(2, half).wait_send()
        for k in range(2, 7):
            sib_copy(k, half).wait_send()
    up_copy(3, 0).wait_send()
    dn_copy(3, 1).wait_send()
    drain_w_out()
    for k in (2, 3, 4, 5, 6):
        for half in (0, 1):
            x_copy(k, 1 + 2 * half).wait_send()
            f_copy(k, half).wait_send()
        y_both(k, lambda copy: copy.wait_send())

    for pair in (0, 1):
        for up in (1, 0):
            ow_copy(pair, up).wait_recv()
        os_copy(pair).start()
    for i in range(3):
        os_copy(i).wait_recv()
    for k in range(8):
        for other in (0, 1):
            if k or other:
                a_wait(k, other).wait_recv()

    for j in range(4):
        cols = pl.ds(j * 512, 512)
        acc = jnp.zeros((128, 512), jnp.float32)
        for cc in range(2):
            for ll in range(2):
                part = wout[cc, ll, :, :, cols].reshape(512, 512)
                acc = acc + jnp.dot(attr[cc * 2 + ll], part, preferred_element_type=jnp.float32)
        out_ref[:, cols] = (
            tok_ref[:, cols].astype(jnp.float32) + gate_ref[:, cols] * acc
        ).astype(jnp.bfloat16)

    for up in (1, 0):
        oz_copy(up).wait_send()
        for pair in (0, 1):
            ow_copy(pair, up).wait_send()
    for i in range(3):
        os_copy(i).wait_send()
    for k in range(8):
        for other in (0, 1):
            if k or other:
                a_copy(k, other).wait_send()


def per_device(tokens, w_qkv, w_out, mod_shift, mod_scale, mod_gate, partners, partner_count):
    vmem = pl.BlockSpec(memory_space=pltpu.VMEM)
    smem = pl.BlockSpec(memory_space=pltpu.SMEM)
    hbm = pl.BlockSpec(memory_space=pl.ANY)
    bf16, f32 = jnp.bfloat16, jnp.float32
    dma = pltpu.SemaphoreType.DMA
    return pl.pallas_call(
        kernel,
        out_shape=jax.ShapeDtypeStruct((128, D), bf16),
        in_specs=[vmem, hbm, hbm, vmem, vmem, vmem, smem, smem],
        out_specs=vmem,
        scratch_shapes=[
            pltpu.VMEM((8, 2, 128, D), bf16),
            pltpu.VMEM((D, 384), bf16),
            pltpu.VMEM((4, 8, 128), f32),
            pltpu.VMEM((8, 256, 128), bf16),
            pltpu.VMEM((2, 10, 256, 256), bf16),
            pltpu.VMEM((4, 3, 2, 256, 256), bf16),
            pltpu.VMEM((8, 256, 128), bf16),
            pltpu.VMEM((4, 128, 512), bf16),
            pltpu.VMEM((2, 2, 4, 128, D), bf16),
            pltpu.VMEM((8, 256, 128), f32),
            pltpu.VMEM((8, 256, 128), f32),
            pltpu.VMEM((8, 256, 128), f32),
            dma((3,)), dma((3,)),
            dma((4, 2)), dma((4, 2)),
            dma((4, 2)), dma((4, 2)),
            dma((8, 2)), dma((8, 2)),
            dma((3, 3)), dma((3,)),
            dma((3, 3)), dma((3, 4)),
            dma((8, 3)), dma((8, 3)),
            dma((8, 2)), dma((8, 2)),
            dma((8, 2)), dma((2, 6)),
            dma((8, 2)), dma((8, 2)),
            dma((3,)), dma((3,)),
            dma((3, 2)), dma((3, 2)),
            dma((2,)), dma((2,)),
            dma((2, 2)), dma((2, 2)),
            dma((3,)), dma((3,)),
            dma((2,)),
        ],
        compiler_params=pltpu.CompilerParams(
            collective_id=0, has_side_effects=True, vmem_limit_bytes=56 * 1024 * 1024
        ),
        cost_estimate=pl.CostEstimate(flops=8_000_000_000, bytes_accessed=30_000_000, transcendentals=7_000_000),
    )(tokens, w_qkv, w_out, mod_shift, mod_scale, mod_gate, partners, partner_count)


def solution(mesh):
    in_specs = (
        P(("view", "seq"), None),
        P(None, "seq"),
        P("seq", None),
        P("view", None),
        P("view", None),
        P("view", None),
        P("view", None),
        P("view"),
    )
    out_specs = P(("view", "seq"), None)
    return jax.shard_map(
        per_device, mesh=mesh, in_specs=in_specs, out_specs=out_specs, check_vma=False
    )
```

```python
import functools

import jax
import jax.numpy as jnp
from jax import lax
from jax.experimental import pallas as pl
from jax.experimental.pallas import tpu as pltpu
from jax.sharding import PartitionSpec as P

HEAD_DIM = 128
FRAME_TOK = 256
D = 2048
EPS = 1e-06
NEG = -1e30
EXP_SCALE = HEAD_DIM ** (-0.5) * 1.4426950408889634
MESH = pl.DeviceIdType.MESH


def kernel(
    tok_ref,
    wq_ref,
    wo_ref,
    shift_ref,
    scale_ref,
    gate_ref,
    partners_ref,
    count_ref,
    out_ref,
    normed,
    wbuf,
    biases,
    qbuf,
    kvw,
    kvx,
    abuf,
    attr,
    wout,
    m_st,
    l_st,
    acc_st,
    bias_s,
    bias_r,
    up_s,
    up_r,
    dn_s,
    dn_r,
    sib_s,
    sib_r,
    wx_s,
    wx_r,
    wy_s,
    wy_r,
    x_s,
    x_r,
    f_s,
    f_r,
    y_s,
    y_r,
    a_s,
    a_r,
    ox_s,
    ox_r,
    oy_s,
    oy_r,
    oz_s,
    oz_r,
    ow_s,
    ow_r,
    os_s,
    os_r,
    loc_s,
):
    w = lax.axis_index("view")
    s = lax.axis_index("seq")
    y, zh = lax.div(w, 4), lax.rem(w, 4)
    zl, x, c = lax.div(s, 8), lax.rem(lax.div(s, 2), 4), lax.rem(s, 2)
    z = zh * 2 + zl
    unit_z = [lax.rem(z + k, 8) for k in range(8)]
    unit_v = [lax.div(u, 2) for u in unit_z]
    unit_f = [lax.rem(u, 2) for u in unit_z]
    next_x = [lax.rem(x + d, 4) for d in range(4)]
    next_y = [lax.rem(y + d, 4) for d in range(4)]
    z_dev = [
        [{"view": y * 4 + v, "seq": f * 8 + x * 2 + cc} for cc in (c, 1 - c)]
        for v, f in zip(unit_v, unit_f)
    ]
    x_dev = [{"view": w, "seq": zl * 8 + xx * 2 + c} for xx in next_x]
    y_dev = [{"view": yy * 4 + zh, "seq": s} for yy in next_y]
    sib = z_dev[0][1]

    def rcopy(src, dst, ss, rs, device):
        return pltpu.make_async_remote_copy(
            src_ref=src, dst_ref=dst, send_sem=ss, recv_sem=rs, device_id=device, device_id_type=MESH
        )

    barrier = pltpu.get_barrier_semaphore()
    peers = [sib] + [p for k in range(1, 8) for p in z_dev[k]] + x_dev[1:] + y_dev[1:]
    for p in peers:
        pl.semaphore_signal(barrier, inc=1, device_id=p, device_id_type=MESH)

    t = tok_ref[...].astype(jnp.float32)
    t = t - jnp.mean(t, axis=1, keepdims=True)
    var = jnp.mean(t * t, axis=1, keepdims=True)
    normed[z, c] = (t * lax.rsqrt(var + EPS) * (1.0 + scale_ref[...]) + shift_ref[...]).astype(jnp.bfloat16)

    pl.semaphore_wait(barrier, len(peers))

    def block(zz, cc, half):
        return normed.at[zz, cc, pl.ds(half * 64, 64)]

    def up_copy(k, half):
        b = block(unit_z[(8 - k) % 8], c, half)
        return rcopy(b, b, up_s.at[k, half], up_r.at[k, half], z_dev[1][0])

    def dn_copy(k, half):
        b = block(unit_z[k], c, half)
        return rcopy(b, b, dn_s.at[k, half], dn_r.at[k, half], z_dev[7][0])

    def sib_copy(k, half):
        b = block(unit_z[k], c, half)
        return rcopy(b, b, sib_s.at[k, half], sib_r.at[k, half], sib)

    for half in (0, 1):
        up_copy(0, half).start()
        dn_copy(0, half).start()
    for half in (0, 1):
        sib_copy(0, half).start()

    def piece(ref, p):
        return ref.at[pl.ds(pl.multiple_of(y * 512, 512), 512), pl.ds(p * 128, 128)]

    native = x == zh

    def wx_copy(p, d):
        return rcopy(piece(wq_ref, p), piece(wbuf, p), wx_s.at[p, d - 1], wx_r.at[p], x_dev[d])

    def wy_copy(p, d):
        return rcopy(piece(wbuf, p), piece(wbuf, p), wy_s.at[p, d - 1], wy_r.at[p, y], y_dev[d])

    def pass_weights(p):
        @pl.when(jnp.logical_not(native))
        def _():
            wx_copy(p, 1).wait_recv()
            for d in (1, 3, 2):
                wy_copy(p, d).start()

    def wait_weights(p):
        @pl.when(jnp.logical_not(native))
        def _():
            for d in range(1, 4):
                rcopy(piece(wbuf, p), piece(wbuf, p), wy_s.at[p, 0], wy_r.at[p, next_y[d]], sib).wait_recv()

    own_w = pltpu.make_async_copy(wq_ref, wbuf, loc_s.at[0])
    own_o = pltpu.make_async_copy(wo_ref, wout.at[c, zl, x], loc_s.at[1])
    own_o.start()

    @pl.when(native)
    def _():
        for p in (1, 2, 0):
            for d in (1, 3, 2):
                wx_copy(p, d).start()
        own_w.start()

    for j in range(7):
        if j != 3:
            target = lax.rem(w + j + 13, 16)
            hits = 0.0
            for slot in range(6):
                hit = jnp.logical_and(partners_ref[0, slot] == target, count_ref[0] > slot)
                hits = hits + jnp.where(hit, 1.0, 0.0)
            biases[zh, j : j + 1, :] = jnp.full((1, 128), jnp.where(hits > 0.0, 0.0, NEG), jnp.float32)
    m_st[...] = jnp.full(m_st.shape, NEG, jnp.float32)
    l_st[...] = jnp.zeros(l_st.shape, jnp.float32)
    acc_st[...] = jnp.zeros(acc_st.shape, jnp.float32)

    def bias_copy(d):
        b = biases.at[zh]
        return rcopy(b, b, bias_s.at[d - 1], bias_r.at[d - 1], z_dev[2 * d][0])

    for d in range(1, 4):
        bias_copy(d).start()

    def event(k, half):
        if k < 4 or half == 0:
            up_copy(k - 1, half).wait_recv()
            if k < 3 or (k == 3 and half == 0):
                up_copy(k, half).start()
        if k < 4 or half == 1:
            dn_copy(k - 1, half).wait_recv()
            if k < 3 or (k == 3 and half == 1):
                dn_copy(k, half).start()
        if k < 4:
            sib_copy(8 - k, half).start()
            sib_copy(k, half).start()
        else:
            sib_copy(4, half).start()

    def x_copy(k, d):
        zz, v, fi = unit_z[k], unit_v[k], unit_f[k]
        return rcopy(kvw.at[fi, 3 + v], kvx.at[v, d - 1, fi], x_s.at[zz, d - 1], x_r.at[zz, d - 1], x_dev[d])

    def f_copy(k, half):
        zz, v, fi = unit_z[k], unit_v[k], unit_f[k]
        rows = pl.ds(half * 128, 128)
        src = kvw.at[fi, 3 + v, rows] if k == 4 else kvx.at[v, 2 * half, fi, rows]
        to = x_dev[2] if k == 4 else x_dev[1 + 2 * half]
        return rcopy(src, kvx.at[v, 1, fi, rows], f_s.at[zz, half], f_r.at[zz, half], to)

    def forward(k):
        for half in (0, 1):
            x_copy(k, 1 + 2 * half).wait_recv()
            f_copy(k, half).start()

    def yup_copy(k):
        zz, v, fi = unit_z[k], unit_v[k], unit_f[k]
        return rcopy(kvw.at[fi, 3 + v], kvw.at[fi, v - 1], y_s.at[zz, 0], y_r.at[fi, v - 1], y_dev[1])

    def ydn_copy(k):
        zz, v, fi = unit_z[k], unit_v[k], unit_f[k]
        return rcopy(kvw.at[fi, 3 + v], kvw.at[fi, 7 + v], y_s.at[zz, 1], y_r.at[fi, 3 + v], y_dev[3])

    def y_both(k, act):
        @pl.when(unit_z[k] >= 2)
        def _():
            act(yup_copy(k))

        @pl.when(unit_z[k] < 6)
        def _():
            act(ydn_copy(k))

    def kv_unit(k):
        for half in (0, 1):
            sib_copy(k, half).wait_recv()
        rows = normed[unit_z[k]].reshape(256, D)
        kv = jnp.dot(rows, wbuf[:, HEAD_DIM:], preferred_element_type=jnp.float32)
        kvw[unit_f[k], 3 + unit_v[k]] = kv.astype(jnp.bfloat16)
        for d in (1, 3):
            x_copy(k, d).start()
        if k == 4:
            for half in (0, 1):
                f_copy(k, half).start()
        y_both(k, lambda copy: copy.start())

    def q_unit(k):
        rows = normed[unit_z[k]].reshape(256, D)
        q = jnp.dot(rows, wbuf[:, :HEAD_DIM], preferred_element_type=jnp.float32)
        qbuf[unit_z[k]] = q.astype(jnp.bfloat16)

    par = lax.rem(y, 2)
    half_rows = pl.ds(pl.multiple_of(par * 64, 64), 64)

    def quarter_rows(up):
        return pl.ds(pl.multiple_of(par * 64 + (1 - up) * 32, 32), 32)

    def ox_copy(d):
        return rcopy(
            wo_ref.at[half_rows], wout.at[c, zl, x, half_rows], ox_s.at[d - 1], ox_r.at[d - 1], x_dev[d]
        )

    def oy_copy(d, up):
        b = wout.at[c, zl, next_x[d], quarter_rows(up)]
        return rcopy(b, b, oy_s.at[d - 1, up], oy_r.at[d - 1, up], y_dev[1 if up else 3])

    def drain_w_out():
        for d in range(1, 4):
            ox_copy(d).wait_send()
            for up in (1, 0):
                oy_copy(d, up).wait_send()

    def oz_copy(up):
        b = wout.at[c, zl, pl.ds((1 - up) * 2, 2), half_rows]
        return rcopy(b, b, oz_s.at[up], oz_r.at[up], z_dev[1 if up else 7][0])

    def ow_copy(pair, up):
        b = wout.at[c, 1 - zl, pl.ds(pair * 2, 2), quarter_rows(up)]
        return rcopy(b, b, ow_s.at[pair, up], ow_r.at[pair, up], y_dev[1 if up else 3])

    def os_copy(i):
        b = wout.at[c, zl] if i == 2 else wout.at[c, 1 - zl, pl.ds(i * 2, 2)]
        return rcopy(b, b, os_s.at[i], os_r.at[i], sib)

    for d in (1, 3, 2):
        ox_copy(d).start()
    pass_weights(1)
    event(1, 0)
    pass_weights(2)
    event(1, 1)
    pass_weights(0)

    @pl.when(native)
    def _():
        for p in range(3):
            for d in range(1, 4):
                wx_copy(p, d).wait_send()
        own_w.wait()

    def acols(cc, ll, xx):
        return attr.at[cc * 2 + ll, :, pl.ds(pl.multiple_of(xx * 128, 128), 128)]

    def a_copy(k, other):
        cc = 1 - c if other else c
        return rcopy(
            abuf.at[unit_z[k], pl.ds(pl.multiple_of(cc * 128, 128), 128)],
            acols(c, zl, zh),
            a_s.at[k, other],
            a_r.at[k, other],
            z_dev[k][other],
        )

    def a_wait(k, other):
        src = acols(1 - c if other else c, unit_f[(8 - k) % 8], unit_v[(8 - k) % 8])
        return rcopy(src, src, a_s.at[k, other], a_r.at[k, other], sib)

    def finish(ks):
        for k in ks:
            u = unit_z[k]
            den = jnp.sum(l_st[u], axis=1, keepdims=True)
            abuf[u] = (acc_st[u] / den).astype(jnp.bfloat16)
        for k in ks:
            if k == 0:
                acols(c, zl, zh)[...] = abuf[z, pl.ds(pl.multiple_of(c * 128, 128), 128)]
            else:
                a_copy(k, 0).start()
            a_copy(k, 1).start()

    def groups(parts):
        first = []
        for u, blocks in parts:
            q = qbuf[u]
            scores = []
            for kv, row in blocks:
                sc = lax.dot_general(
                    q, kv[:, :HEAD_DIM], (((1,), (1,)), ((), ())), preferred_element_type=jnp.float32
                )
                if row is not None:
                    b = biases[lax.div(u, 2), pl.ds(row, 1), :]
                    sc = sc + jnp.concatenate([b, b], axis=1)
                scores.append(sc)
            mx = functools.reduce(jnp.maximum, scores)
            mx = jnp.max(mx, axis=1, keepdims=True) * EXP_SCALE
            m_old = m_st[u]
            m_new = jnp.maximum(m_old, mx)
            first.append((scores, m_new, jnp.exp2(m_old - m_new)))
        second = []
        for (u, blocks), (scores, m_new, alpha) in zip(parts, first):
            m_two = jnp.concatenate([m_new, m_new], axis=1)
            total = jnp.zeros((256, 256), jnp.float32)
            acc = jnp.zeros((256, HEAD_DIM), jnp.float32)
            for sc, (kv, row) in zip(scores, blocks):
                p = jnp.exp2(sc * EXP_SCALE - m_two)
                total = total + p
                acc = acc + jnp.dot(
                    p.astype(jnp.bfloat16), kv[:, HEAD_DIM:], preferred_element_type=jnp.float32
                )
            second.append((total, acc))
        for (u, blocks), (scores, m_new, alpha), (total, acc) in zip(parts, first, second):
            m_st[u] = m_new
            l_st[u] = l_st[u] * alpha + total[:, :128] + total[:, 128:]
            acc_st[u] = acc_st[u] * alpha + acc

    def own_view(v):
        parts = []
        for fi in range(2):
            blocks = [(kvw.at[fi, 3 + v], None), (kvw.at[1 - fi, 3 + v], None)]
            blocks += [(kvx.at[v, d, f], None) for d in range(3) for f in range(2)]
            parts.append((2 * v + fi, blocks))
        groups(parts)

    def last_view(late):
        parts = []
        for fi in range(2):
            blocks = [(kvx.at[view_d, d, zl if late else 1 - zl], None) for d in range(3)]
            if not late:
                blocks += [(kvw.at[fi, 3 + view_d], None), (kvw.at[1 - fi, 3 + view_d], None)]
            parts.append((2 * view_d + fi, blocks))
        groups(parts)

    def window(v, fi, deltas):
        blocks = [(kvw.at[fi, v + o], o) for delta in deltas for o in (delta - 1, delta + 3)]
        return 2 * v + fi, blocks

    def wait_x(k):
        for half in (0, 1):
            f_copy(k, half).wait_recv()
        if k == 4:
            for half in (0, 1):
                x_copy(k, 1 + 2 * half).wait_recv()

    def wait_y(k):
        y_both(k, lambda copy: copy.wait_recv())

    sign = 1 - 2 * zl
    view_b, view_c, view_d = lax.rem(zh + 4 - sign, 4), lax.rem(zh + 4 + sign, 4), unit_v[4]
    views = [unit_v[6], zh, unit_v[2]]
    gaps = [3, 2, 1]

    wait_weights(1)
    wait_weights(2)
    kv_unit(0)
    event(2, 0)
    kv_unit(1)
    kv_unit(7)
    wait_weights(0)
    for d in range(1, 4):
        ox_copy(d).wait_recv()
    for d in range(1, 4):
        for up in (1, 0):
            oy_copy(d, up).start()
    event(2, 1)
    kv_unit(2)
    kv_unit(6)
    for k in (0, 1, 7):
        q_unit(k)
    forward(0)
    event(3, 0)
    q_unit(2)
    q_unit(6)
    forward(1)
    forward(7)
    for half in (0, 1):
        for k in range(2):
            up_copy(k, half).wait_send()
            dn_copy(k, half).wait_send()
        for k in (0, 1, 7):
            sib_copy(k, half).wait_send()
    for d in range(1, 4):
        bias_copy(d).wait_send()
        bias_copy(d).wait_recv()

    @pl.when(jnp.logical_not(native))
    def _():
        for p in range(3):
            for d in range(1, 4):
                wy_copy(p, d).wait_send()

    event(3, 1)
    for d in range(1, 4):
        for up in (1, 0):
            oy_copy(d, up).wait_recv()
    own_o.wait()
    for up in (1, 0):
        oz_copy(up).start()
    kv_unit(3)
    kv_unit(5)
    q_unit(3)
    q_unit(5)
    forward(2)
    forward(6)
    for k in (0, 1, 7):
        wait_x(k)
    own_view(zh)
    for k in (0, 1, 7):
        for half in (0, 1):
            x_copy(k, 1 + 2 * half).wait_send()
            f_copy(k, half).wait_send()
        y_both(k, lambda copy: copy.wait_send())
    event(4, 0)
    event(4, 1)
    kv_unit(4)
    forward(3)
    forward(5)
    q_unit(4)
    os_copy(2).start()
    wait_x(2)
    wait_x(6)
    own_view(view_b)
    for pair in (0, 1):
        oz_copy(1 - pair).wait_recv()
        for up in (1, 0):
            ow_copy(pair, up).start()
    for k in (1, 7, 3, 5):
        wait_y(k)
    groups([window(unit_v[k], 1 - zl, (1, 2, 3)) for k in (1, 3, 5, 7)])
    finish((1, 7))
    for k in (0, 2, 6):
        wait_y(k)
    groups([window(v, zl, [e for e in (1, 2, 3) if e != g]) for v, g in zip(views, gaps)])
    wait_y(4)
    groups(
        [window(v, zl, (g,)) for v, g in zip(views, gaps)] + [window(view_d, zl, (1, 2, 3))]
    )
    wait_x(3)
    wait_x(5)
    own_view(view_c)
    finish((0, 2, 6))

    @pl.when(zl == 0)
    def _():
        finish((3,))

    @pl.when(zl == 1)
    def _():
        finish((5,))

    last_view(False)
    wait_x(4)
    last_view(True)

    @pl.when(zl == 0)
    def _():
        finish((5,))

    @pl.when(zl == 1)
    def _():
        finish((3,))

    finish((4,))

    for half in (0, 1):
        up_copy(2, half).wait_send()
        dn_copy(2, half).wait_send()
        for k in range(2, 7):
            sib_copy(k, half).wait_send()
    up_copy(3, 0).wait_send()
    dn_copy(3, 1).wait_send()
    drain_w_out()
    for k in (2, 3, 4, 5, 6):
        for half in (0, 1):
            x_copy(k, 1 + 2 * half).wait_send()
            f_copy(k, half).wait_send()
        y_both(k, lambda copy: copy.wait_send())

    for pair in (0, 1):
        for up in (1, 0):
            ow_copy(pair, up).wait_recv()
        os_copy(pair).start()
    for i in range(3):
        os_copy(i).wait_recv()
    for k in range(8):
        for other in (0, 1):
            if k or other:
                a_wait(k, other).wait_recv()

    for j in range(4):
        cols = pl.ds(j * 512, 512)
        acc = jnp.zeros((128, 512), jnp.float32)
        for cc in range(2):
            for ll in range(2):
                part = wout[cc, ll, :, :, cols].reshape(512, 512)
                acc = acc + jnp.dot(attr[cc * 2 + ll], part, preferred_element_type=jnp.float32)
        out_ref[:, cols] = (
            tok_ref[:, cols].astype(jnp.float32) + gate_ref[:, cols] * acc
        ).astype(jnp.bfloat16)

    for up in (1, 0):
        oz_copy(up).wait_send()
        for pair in (0, 1):
            ow_copy(pair, up).wait_send()
    for i in range(3):
        os_copy(i).wait_send()
    for k in range(8):
        for other in (0, 1):
            if k or other:
                a_copy(k, other).wait_send()


def per_device(tokens, w_qkv, w_out, mod_shift, mod_scale, mod_gate, partners, partner_count):
    vmem = pl.BlockSpec(memory_space=pltpu.VMEM)
    smem = pl.BlockSpec(memory_space=pltpu.SMEM)
    hbm = pl.BlockSpec(memory_space=pl.ANY)
    bf16, f32 = jnp.bfloat16, jnp.float32
    dma = pltpu.SemaphoreType.DMA
    return pl.pallas_call(
        kernel,
        out_shape=jax.ShapeDtypeStruct((128, D), bf16),
        in_specs=[vmem, hbm, hbm, vmem, vmem, vmem, smem, smem],
        out_specs=vmem,
        scratch_shapes=[
            pltpu.VMEM((8, 2, 128, D), bf16),
            pltpu.VMEM((D, 384), bf16),
            pltpu.VMEM((4, 8, 128), f32),
            pltpu.VMEM((8, 256, 128), bf16),
            pltpu.VMEM((2, 10, 256, 256), bf16),
            pltpu.VMEM((4, 3, 2, 256, 256), bf16),
            pltpu.VMEM((8, 256, 128), bf16),
            pltpu.VMEM((4, 128, 512), bf16),
            pltpu.VMEM((2, 2, 4, 128, D), bf16),
            pltpu.VMEM((8, 256, 128), f32),
            pltpu.VMEM((8, 256, 128), f32),
            pltpu.VMEM((8, 256, 128), f32),
            dma((3,)), dma((3,)),
            dma((4, 2)), dma((4, 2)),
            dma((4, 2)), dma((4, 2)),
            dma((8, 2)), dma((8, 2)),
            dma((3, 3)), dma((3,)),
            dma((3, 3)), dma((3, 4)),
            dma((8, 3)), dma((8, 3)),
            dma((8, 2)), dma((8, 2)),
            dma((8, 2)), dma((2, 6)),
            dma((8, 2)), dma((8, 2)),
            dma((3,)), dma((3,)),
            dma((3, 2)), dma((3, 2)),
            dma((2,)), dma((2,)),
            dma((2, 2)), dma((2, 2)),
            dma((3,)), dma((3,)),
            dma((2,)),
        ],
        compiler_params=pltpu.CompilerParams(
            collective_id=0, has_side_effects=True, vmem_limit_bytes=56 * 1024 * 1024
        ),
        cost_estimate=pl.CostEstimate(flops=8_000_000_000, bytes_accessed=30_000_000, transcendentals=7_000_000),
    )(tokens, w_qkv, w_out, mod_shift, mod_scale, mod_gate, partners, partner_count)


def solution(mesh):
    in_specs = (
        P(("view", "seq"), None),
        P(None, "seq"),
        P("seq", None),
        P("view", None),
        P("view", None),
        P("view", None),
        P("view", None),
        P("view"),
    )
    out_specs = P(("view", "seq"), None)
    return jax.shard_map(
        per_device, mesh=mesh, in_specs=in_specs, out_specs=out_specs, check_vma=False
    )
```

```python
import functools

import jax
import jax.numpy as jnp
from jax import lax
from jax.experimental import pallas as pl
from jax.experimental.pallas import tpu as pltpu
from jax.sharding import PartitionSpec as P

HEAD_DIM = 128
FRAME_TOK = 256
D = 2048
EPS = 1e-06
NEG = -1e30
EXP_SCALE = HEAD_DIM ** (-0.5) * 1.4426950408889634
MESH = pl.DeviceIdType.MESH


def kernel(
    tok_ref,
    wq_ref,
    wo_ref,
    shift_ref,
    scale_ref,
    gate_ref,
    partners_ref,
    count_ref,
    out_ref,
    normed,
    wbuf,
    biases,
    qbuf,
    kvw,
    kvx,
    abuf,
    attr,
    wout,
    m_st,
    l_st,
    acc_st,
    bias_s,
    bias_r,
    up_s,
    up_r,
    dn_s,
    dn_r,
    sib_s,
    sib_r,
    wx_s,
    wx_r,
    wy_s,
    wy_r,
    x_s,
    x_r,
    f_s,
    f_r,
    y_s,
    y_r,
    a_s,
    a_r,
    ox_s,
    ox_r,
    of_s,
    of_r,
    oy_s,
    oy_r,
    oz_s,
    oz_r,
    ow_s,
    ow_r,
    os_s,
    os_r,
    loc_s,
):
    w = lax.axis_index("view")
    s = lax.axis_index("seq")
    y, zh = lax.div(w, 4), lax.rem(w, 4)
    zl, x, c = lax.div(s, 8), lax.rem(lax.div(s, 2), 4), lax.rem(s, 2)
    z = zh * 2 + zl
    unit_z = [lax.rem(z + k, 8) for k in range(8)]
    unit_v = [lax.div(u, 2) for u in unit_z]
    unit_f = [lax.rem(u, 2) for u in unit_z]
    next_x = [lax.rem(x + d, 4) for d in range(4)]
    next_y = [lax.rem(y + d, 4) for d in range(4)]
    z_dev = [
        [{"view": y * 4 + v, "seq": f * 8 + x * 2 + cc} for cc in (c, 1 - c)]
        for v, f in zip(unit_v, unit_f)
    ]
    x_dev = [{"view": w, "seq": zl * 8 + xx * 2 + c} for xx in next_x]
    y_dev = [{"view": yy * 4 + zh, "seq": s} for yy in next_y]
    sib = z_dev[0][1]

    def rcopy(src, dst, ss, rs, device):
        return pltpu.make_async_remote_copy(
            src_ref=src, dst_ref=dst, send_sem=ss, recv_sem=rs, device_id=device, device_id_type=MESH
        )

    barrier = pltpu.get_barrier_semaphore()
    peers = [sib] + [p for k in range(1, 8) for p in z_dev[k]] + x_dev[1:] + y_dev[1:]
    for p in peers:
        pl.semaphore_signal(barrier, inc=1, device_id=p, device_id_type=MESH)

    t = tok_ref[...].astype(jnp.float32)
    t = t - jnp.mean(t, axis=1, keepdims=True)
    var = jnp.mean(t * t, axis=1, keepdims=True)
    normed[z, c] = (t * lax.rsqrt(var + EPS) * (1.0 + scale_ref[...]) + shift_ref[...]).astype(jnp.bfloat16)

    pl.semaphore_wait(barrier, len(peers))

    def block(zz, cc, half):
        return normed.at[zz, cc, pl.ds(half * 64, 64)]

    def up_copy(k, half):
        b = block(unit_z[(8 - k) % 8], c, half)
        return rcopy(b, b, up_s.at[k, half], up_r.at[k, half], z_dev[1][0])

    def dn_copy(k, half):
        b = block(unit_z[k], c, half)
        return rcopy(b, b, dn_s.at[k, half], dn_r.at[k, half], z_dev[7][0])

    def sib_copy(k, half):
        b = block(unit_z[k], c, half)
        return rcopy(b, b, sib_s.at[k, half], sib_r.at[k, half], sib)

    for half in (0, 1):
        up_copy(0, half).start()
        dn_copy(0, half).start()
    for half in (0, 1):
        sib_copy(0, half).start()

    def piece(ref, p):
        return ref.at[pl.ds(pl.multiple_of(y * 512, 512), 512), pl.ds(p * 128, 128)]

    native = x == zh

    def wx_copy(p, d):
        return rcopy(piece(wq_ref, p), piece(wbuf, p), wx_s.at[p, d - 1], wx_r.at[p], x_dev[d])

    def wy_copy(p, d):
        return rcopy(piece(wbuf, p), piece(wbuf, p), wy_s.at[p, d - 1], wy_r.at[p, y], y_dev[d])

    def pass_weights(p):
        @pl.when(jnp.logical_not(native))
        def _():
            wx_copy(p, 1).wait_recv()
            for d in (1, 3, 2):
                wy_copy(p, d).start()

    def wait_weights(p):
        @pl.when(jnp.logical_not(native))
        def _():
            for d in range(1, 4):
                rcopy(piece(wbuf, p), piece(wbuf, p), wy_s.at[p, 0], wy_r.at[p, next_y[d]], sib).wait_recv()

    own_w = pltpu.make_async_copy(wq_ref, wbuf, loc_s.at[0])
    own_o = pltpu.make_async_copy(wo_ref, wout.at[c, zl, x], loc_s.at[1])
    own_o.start()

    @pl.when(native)
    def _():
        for p in (1, 2, 0):
            for d in (1, 3, 2):
                wx_copy(p, d).start()
        own_w.start()

    for j in range(7):
        if j != 3:
            target = lax.rem(w + j + 13, 16)
            hits = 0.0
            for slot in range(6):
                hit = jnp.logical_and(partners_ref[0, slot] == target, count_ref[0] > slot)
                hits = hits + jnp.where(hit, 1.0, 0.0)
            biases[zh, j : j + 1, :] = jnp.full((1, 128), jnp.where(hits > 0.0, 0.0, NEG), jnp.float32)
    m_st[...] = jnp.full(m_st.shape, NEG, jnp.float32)
    l_st[...] = jnp.zeros(l_st.shape, jnp.float32)
    acc_st[...] = jnp.zeros(acc_st.shape, jnp.float32)

    def bias_copy(d):
        b = biases.at[zh]
        return rcopy(b, b, bias_s.at[d - 1], bias_r.at[d - 1], z_dev[2 * d][0])

    for d in range(1, 4):
        bias_copy(d).start()

    def event(k, half):
        if k < 4 or half == 0:
            up_copy(k - 1, half).wait_recv()
            if k < 3 or (k == 3 and half == 0):
                up_copy(k, half).start()
        if k < 4 or half == 1:
            dn_copy(k - 1, half).wait_recv()
            if k < 3 or (k == 3 and half == 1):
                dn_copy(k, half).start()
        if k < 4:
            sib_copy(8 - k, half).start()
            sib_copy(k, half).start()
        else:
            sib_copy(4, half).start()

    def x_copy(k, d):
        zz, v, fi = unit_z[k], unit_v[k], unit_f[k]
        return rcopy(kvw.at[fi, 3 + v], kvx.at[v, d - 1, fi], x_s.at[zz, d - 1], x_r.at[zz, d - 1], x_dev[d])

    def f_copy(k, half):
        zz, v, fi = unit_z[k], unit_v[k], unit_f[k]
        rows = pl.ds(half * 128, 128)
        src = kvw.at[fi, 3 + v, rows] if k == 4 else kvx.at[v, 2 * half, fi, rows]
        to = x_dev[2] if k == 4 else x_dev[1 + 2 * half]
        return rcopy(src, kvx.at[v, 1, fi, rows], f_s.at[zz, half], f_r.at[zz, half], to)

    def forward(k):
        for half in (0, 1):
            x_copy(k, 1 + 2 * half).wait_recv()
            f_copy(k, half).start()

    def yup_copy(k):
        zz, v, fi = unit_z[k], unit_v[k], unit_f[k]
        return rcopy(kvw.at[fi, 3 + v], kvw.at[fi, v - 1], y_s.at[zz, 0], y_r.at[fi, v - 1], y_dev[1])

    def ydn_copy(k):
        zz, v, fi = unit_z[k], unit_v[k], unit_f[k]
        return rcopy(kvw.at[fi, 3 + v], kvw.at[fi, 7 + v], y_s.at[zz, 1], y_r.at[fi, 3 + v], y_dev[3])

    def y_both(k, act):
        @pl.when(unit_z[k] >= 2)
        def _():
            act(yup_copy(k))

        @pl.when(unit_z[k] < 6)
        def _():
            act(ydn_copy(k))

    def kv_unit(k):
        for half in (0, 1):
            sib_copy(k, half).wait_recv()
        rows = normed[unit_z[k]].reshape(256, D)
        kv = jnp.dot(rows, wbuf[:, HEAD_DIM:], preferred_element_type=jnp.float32)
        kvw[unit_f[k], 3 + unit_v[k]] = kv.astype(jnp.bfloat16)
        for d in (1, 3):
            x_copy(k, d).start()
        if k == 4:
            for half in (0, 1):
                f_copy(k, half).start()
        y_both(k, lambda copy: copy.start())

    def q_unit(k):
        rows = normed[unit_z[k]].reshape(256, D)
        q = jnp.dot(rows, wbuf[:, :HEAD_DIM], preferred_element_type=jnp.float32)
        qbuf[unit_z[k]] = q.astype(jnp.bfloat16)

    par = lax.rem(y, 2)
    half_rows = pl.ds(pl.multiple_of(par * 64, 64), 64)

    def quarter_rows(up):
        return pl.ds(pl.multiple_of(par * 64 + (1 - up) * 32, 32), 32)

    def ox_copy(d):
        return rcopy(
            wo_ref.at[half_rows], wout.at[c, zl, x, half_rows], ox_s.at[d - 1], ox_r.at[d - 1], x_dev[d]
        )

    def of_copy(i):
        b = wout.at[c, zl, next_x[3 - 2 * i], quarter_rows(1 - i)]
        return rcopy(b, b, of_s.at[i], of_r.at[i], x_dev[1 + 2 * i])

    def oy_copy(d, up):
        b = wout.at[c, zl, next_x[d], quarter_rows(up)]
        return rcopy(b, b, oy_s.at[d - 1, up], oy_r.at[d - 1, up], y_dev[1 if up else 3])

    def drain_w_out():
        for i in (0, 1):
            of_copy(i).wait_send()
        for d in range(1, 4):
            if d != 2:
                ox_copy(d).wait_send()
            for up in (1, 0):
                oy_copy(d, up).wait_send()

    def oz_copy(up):
        b = wout.at[c, zl, pl.ds((1 - up) * 2, 2), half_rows]
        return rcopy(b, b, oz_s.at[up], oz_r.at[up], z_dev[1 if up else 7][0])

    def ow_copy(pair, up):
        b = wout.at[c, 1 - zl, pl.ds(pair * 2, 2), quarter_rows(up)]
        return rcopy(b, b, ow_s.at[pair, up], ow_r.at[pair, up], y_dev[1 if up else 3])

    def os_copy(i):
        b = wout.at[c, zl] if i == 2 else wout.at[c, 1 - zl, pl.ds(i * 2, 2)]
        return rcopy(b, b, os_s.at[i], os_r.at[i], sib)

    for d in (1, 3):
        ox_copy(d).start()
    pass_weights(1)
    event(1, 0)
    pass_weights(2)
    event(1, 1)
    pass_weights(0)

    @pl.when(native)
    def _():
        for p in range(3):
            for d in range(1, 4):
                wx_copy(p, d).wait_send()
        own_w.wait()

    def acols(cc, ll, xx):
        return attr.at[cc * 2 + ll, :, pl.ds(pl.multiple_of(xx * 128, 128), 128)]

    def a_copy(k, other):
        cc = 1 - c if other else c
        return rcopy(
            abuf.at[unit_z[k], pl.ds(pl.multiple_of(cc * 128, 128), 128)],
            acols(c, zl, zh),
            a_s.at[k, other],
            a_r.at[k, other],
            z_dev[k][other],
        )

    def a_wait(k, other):
        src = acols(1 - c if other else c, unit_f[(8 - k) % 8], unit_v[(8 - k) % 8])
        return rcopy(src, src, a_s.at[k, other], a_r.at[k, other], sib)

    def finish(ks):
        for k in ks:
            u = unit_z[k]
            den = jnp.sum(l_st[u], axis=1, keepdims=True)
            abuf[u] = (acc_st[u] / den).astype(jnp.bfloat16)
        for k in ks:
            if k == 0:
                acols(c, zl, zh)[...] = abuf[z, pl.ds(pl.multiple_of(c * 128, 128), 128)]
            else:
                a_copy(k, 0).start()
            a_copy(k, 1).start()

    def groups(parts):
        first = []
        for u, blocks in parts:
            q = qbuf[u]
            scores = []
            for kv, row in blocks:
                sc = lax.dot_general(
                    q, kv[:, :HEAD_DIM], (((1,), (1,)), ((), ())), preferred_element_type=jnp.float32
                )
                if row is not None:
                    b = biases[lax.div(u, 2), pl.ds(row, 1), :]
                    sc = sc + jnp.concatenate([b, b], axis=1)
                scores.append(sc)
            mx = functools.reduce(jnp.maximum, scores)
            mx = jnp.max(mx, axis=1, keepdims=True) * EXP_SCALE
            m_old = m_st[u]
            m_new = jnp.maximum(m_old, mx)
            first.append((scores, m_new, jnp.exp2(m_old - m_new)))
        second = []
        for (u, blocks), (scores, m_new, alpha) in zip(parts, first):
            m_two = jnp.concatenate([m_new, m_new], axis=1)
            total = jnp.zeros((256, 256), jnp.float32)
            acc = jnp.zeros((256, HEAD_DIM), jnp.float32)
            for sc, (kv, row) in zip(scores, blocks):
                p = jnp.exp2(sc * EXP_SCALE - m_two)
                total = total + p
                acc = acc + jnp.dot(
                    p.astype(jnp.bfloat16), kv[:, HEAD_DIM:], preferred_element_type=jnp.float32
                )
            second.append((total, acc))
        for (u, blocks), (scores, m_new, alpha), (total, acc) in zip(parts, first, second):
            m_st[u] = m_new
            l_st[u] = l_st[u] * alpha + total[:, :128] + total[:, 128:]
            acc_st[u] = acc_st[u] * alpha + acc

    def own_view(v):
        parts = []
        for fi in range(2):
            blocks = [(kvw.at[fi, 3 + v], None), (kvw.at[1 - fi, 3 + v], None)]
            blocks += [(kvx.at[v, d, f], None) for d in range(3) for f in range(2)]
            parts.append((2 * v + fi, blocks))
        groups(parts)

    def last_view(late):
        parts = []
        for fi in range(2):
            blocks = [(kvx.at[view_d, d, zl if late else 1 - zl], None) for d in range(3)]
            if not late:
                blocks += [(kvw.at[fi, 3 + view_d], None), (kvw.at[1 - fi, 3 + view_d], None)]
            parts.append((2 * view_d + fi, blocks))
        groups(parts)

    def window(v, fi, deltas):
        blocks = [(kvw.at[fi, v + o], o) for delta in deltas for o in (delta - 1, delta + 3)]
        return 2 * v + fi, blocks

    def wait_x(k):
        for half in (0, 1):
            f_copy(k, half).wait_recv()
        if k == 4:
            for half in (0, 1):
                x_copy(k, 1 + 2 * half).wait_recv()

    def wait_y(k):
        y_both(k, lambda copy: copy.wait_recv())

    sign = 1 - 2 * zl
    view_b, view_c, view_d = lax.rem(zh + 4 - sign, 4), lax.rem(zh + 4 + sign, 4), unit_v[4]
    views = [unit_v[6], zh, unit_v[2]]
    gaps = [3, 2, 1]

    wait_weights(1)
    wait_weights(2)
    kv_unit(0)
    for i in (0, 1):
        ox_copy(1 + 2 * i).wait_recv()
        of_copy(i).start()
    event(2, 0)
    kv_unit(1)
    kv_unit(7)
    wait_weights(0)
    for i in (0, 1):
        of_copy(i).wait_recv()
    for d in range(1, 4):
        for up in (1, 0):
            oy_copy(d, up).start()
    event(2, 1)
    kv_unit(2)
    kv_unit(6)
    for k in (0, 1, 7):
        q_unit(k)
    forward(0)
    event(3, 0)
    q_unit(2)
    q_unit(6)
    forward(1)
    forward(7)
    for half in (0, 1):
        for k in range(2):
            up_copy(k, half).wait_send()
            dn_copy(k, half).wait_send()
        for k in (0, 1, 7):
            sib_copy(k, half).wait_send()
    for d in range(1, 4):
        bias_copy(d).wait_send()
        bias_copy(d).wait_recv()

    @pl.when(jnp.logical_not(native))
    def _():
        for p in range(3):
            for d in range(1, 4):
                wy_copy(p, d).wait_send()

    event(3, 1)
    for d in range(1, 4):
        for up in (1, 0):
            oy_copy(d, up).wait_recv()
    own_o.wait()
    for up in (1, 0):
        oz_copy(up).start()
    kv_unit(3)
    kv_unit(5)
    q_unit(3)
    q_unit(5)
    forward(2)
    forward(6)
    for k in (0, 1, 7):
        wait_x(k)
    own_view(zh)
    for k in (0, 1, 7):
        for half in (0, 1):
            x_copy(k, 1 + 2 * half).wait_send()
            f_copy(k, half).wait_send()
        y_both(k, lambda copy: copy.wait_send())
    event(4, 0)
    event(4, 1)
    kv_unit(4)
    forward(3)
    forward(5)
    q_unit(4)
    os_copy(2).start()
    wait_x(2)
    wait_x(6)
    own_view(view_b)
    for pair in (0, 1):
        oz_copy(1 - pair).wait_recv()
        for up in (1, 0):
            ow_copy(pair, up).start()
    for k in (1, 7, 3, 5):
        wait_y(k)
    groups([window(unit_v[k], 1 - zl, (1, 2, 3)) for k in (1, 3, 5, 7)])
    finish((1, 7))
    for k in (0, 2, 6):
        wait_y(k)
    groups([window(v, zl, [e for e in (1, 2, 3) if e != g]) for v, g in zip(views, gaps)])
    wait_y(4)
    groups(
        [window(v, zl, (g,)) for v, g in zip(views, gaps)] + [window(view_d, zl, (1, 2, 3))]
    )
    wait_x(3)
    wait_x(5)
    own_view(view_c)
    finish((0, 2, 6))

    @pl.when(zl == 0)
    def _():
        finish((3,))

    @pl.when(zl == 1)
    def _():
        finish((5,))

    last_view(False)
    wait_x(4)
    last_view(True)

    @pl.when(zl == 0)
    def _():
        finish((5,))

    @pl.when(zl == 1)
    def _():
        finish((3,))

    finish((4,))

    for half in (0, 1):
        up_copy(2, half).wait_send()
        dn_copy(2, half).wait_send()
        for k in range(2, 7):
            sib_copy(k, half).wait_send()
    up_copy(3, 0).wait_send()
    dn_copy(3, 1).wait_send()
    drain_w_out()
    for k in (2, 3, 4, 5, 6):
        for half in (0, 1):
            x_copy(k, 1 + 2 * half).wait_send()
            f_copy(k, half).wait_send()
        y_both(k, lambda copy: copy.wait_send())

    for pair in (0, 1):
        for up in (1, 0):
            ow_copy(pair, up).wait_recv()
        os_copy(pair).start()
    for i in range(3):
        os_copy(i).wait_recv()
    for k in range(8):
        for other in (0, 1):
            if k or other:
                a_wait(k, other).wait_recv()

    for j in range(4):
        cols = pl.ds(j * 512, 512)
        acc = jnp.zeros((128, 512), jnp.float32)
        for cc in range(2):
            for ll in range(2):
                part = wout[cc, ll, :, :, cols].reshape(512, 512)
                acc = acc + jnp.dot(attr[cc * 2 + ll], part, preferred_element_type=jnp.float32)
        out_ref[:, cols] = (
            tok_ref[:, cols].astype(jnp.float32) + gate_ref[:, cols] * acc
        ).astype(jnp.bfloat16)

    for up in (1, 0):
        oz_copy(up).wait_send()
        for pair in (0, 1):
            ow_copy(pair, up).wait_send()
    for i in range(3):
        os_copy(i).wait_send()
    for k in range(8):
        for other in (0, 1):
            if k or other:
                a_copy(k, other).wait_send()


def per_device(tokens, w_qkv, w_out, mod_shift, mod_scale, mod_gate, partners, partner_count):
    vmem = pl.BlockSpec(memory_space=pltpu.VMEM)
    smem = pl.BlockSpec(memory_space=pltpu.SMEM)
    hbm = pl.BlockSpec(memory_space=pl.ANY)
    bf16, f32 = jnp.bfloat16, jnp.float32
    dma = pltpu.SemaphoreType.DMA
    return pl.pallas_call(
        kernel,
        out_shape=jax.ShapeDtypeStruct((128, D), bf16),
        in_specs=[vmem, hbm, hbm, vmem, vmem, vmem, smem, smem],
        out_specs=vmem,
        scratch_shapes=[
            pltpu.VMEM((8, 2, 128, D), bf16),
            pltpu.VMEM((D, 384), bf16),
            pltpu.VMEM((4, 8, 128), f32),
            pltpu.VMEM((8, 256, 128), bf16),
            pltpu.VMEM((2, 10, 256, 256), bf16),
            pltpu.VMEM((4, 3, 2, 256, 256), bf16),
            pltpu.VMEM((8, 256, 128), bf16),
            pltpu.VMEM((4, 128, 512), bf16),
            pltpu.VMEM((2, 2, 4, 128, D), bf16),
            pltpu.VMEM((8, 256, 128), f32),
            pltpu.VMEM((8, 256, 128), f32),
            pltpu.VMEM((8, 256, 128), f32),
            dma((3,)), dma((3,)),
            dma((4, 2)), dma((4, 2)),
            dma((4, 2)), dma((4, 2)),
            dma((8, 2)), dma((8, 2)),
            dma((3, 3)), dma((3,)),
            dma((3, 3)), dma((3, 4)),
            dma((8, 3)), dma((8, 3)),
            dma((8, 2)), dma((8, 2)),
            dma((8, 2)), dma((2, 6)),
            dma((8, 2)), dma((8, 2)),
            dma((3,)), dma((3,)),
            dma((2,)), dma((2,)),
            dma((3, 2)), dma((3, 2)),
            dma((2,)), dma((2,)),
            dma((2, 2)), dma((2, 2)),
            dma((3,)), dma((3,)),
            dma((2,)),
        ],
        compiler_params=pltpu.CompilerParams(
            collective_id=0, has_side_effects=True, vmem_limit_bytes=56 * 1024 * 1024
        ),
        cost_estimate=pl.CostEstimate(flops=8_000_000_000, bytes_accessed=30_000_000, transcendentals=7_000_000),
    )(tokens, w_qkv, w_out, mod_shift, mod_scale, mod_gate, partners, partner_count)


def solution(mesh):
    in_specs = (
        P(("view", "seq"), None),
        P(None, "seq"),
        P("seq", None),
        P("view", None),
        P("view", None),
        P("view", None),
        P("view", None),
        P("view"),
    )
    out_specs = P(("view", "seq"), None)
    return jax.shard_map(
        per_device, mesh=mesh, in_specs=in_specs, out_specs=out_specs, check_vma=False
    )
```
